256 devices in a mesh: dp: 2 (over x_hi), tm: 16 (over x_lo, z), space: 8 (over y, core).
Axes of the slice: x: 4 (x_hi: 2, x_lo: 2; x = x_hi * 2 + x_lo), y: 4, z: 8, core: 2. Of those that a mesh axis runs over, the one named last changes fastest.
Arguments:
- tokens: bfloat16 [2, 16, 1024, 1152], P('dp', 'tm', 'space'), may hold values from -6 to 6
- validity: int32 [1024], replicated, may hold values from 0 to 1, as said below
- table_space: float32 [3, 1152], replicated, may hold values from -3 to 3
- qkv_space: bfloat16 [1152, 1728], replicated, may hold values from -0.6 to 0.6
- gains_space: float32 [2, 72], replicated, may hold values from 0.5 to 6
- out_space: bfloat16 [576, 1152], replicated, may hold values from -0.25 to 0.25
- table_time: float32 [3, 1152], replicated, may hold values from -3 to 3
- qkv_time: bfloat16 [1152, 1728], replicated, may hold values from -0.6 to 0.6
- gains_time: float32 [2, 72], replicated, may hold values from 0.5 to 6
- out_time: bfloat16 [576, 1152], replicated, may hold values from -0.25 to 0.25
- cotangent: bfloat16 [2, 16, 1024, 1152], P('dp', 'tm', 'space'), may hold values from -6 to 6
Outputs:
- mixed: bfloat16 [2, 16, 1024, 1152], P('dp', 'tm', 'space')
- token_grad: bfloat16 [2, 16, 1024, 1152], P('dp', 'tm', 'space')
- grad_out_space: float32 [576, 1152], P('space', ('dp', 'tm'))
- grad_out_time: float32 [576, 1152], P('space', ('dp', 'tm'))
- grad_tables: float32 [2, 3, 1152], replicated
The draws below stay inside these ranges and needn't reach their ends.
Inputs may be any that keep to these rules, and one draw needn't show every extreme that they name: `validity`: exactly 1014 of the 1024 entries are 1.
All inputs are finite; a program needn't handle non-finite values.
Results may differ from the reference program's by a relative error of at most 0.03.
Values may be sent and summed in bfloat16 or wider, within the bound.
A program may use at most 128 MiB of HBM per device.

```python
import jax
import jax.numpy as jnp
from jax import lax

D = 1152
HEADS = 8
HEAD_DIM = 72
PATCHES = 1024
VALID = 1014
FRAMES = 16
VIDEOS = 2


def draw_validity(key, part):
    key = jax.random.fold_in(key, 3)
    order = jax.random.permutation(key, PATCHES)
    return (order < VALID).astype(jnp.int32)


def gain_draw(key, lowest, highest):
    spread = jax.random.uniform(key, (2, HEAD_DIM), jnp.float32, jnp.log(lowest), jnp.log(highest))
    return jnp.exp(spread).astype(jnp.float32)


def qkv_draw(key):
    base = jax.random.normal(key, (D, HEADS, 3, HEAD_DIM), jnp.float32)
    paired = base[:, :, 1:2, :]
    base = jnp.concatenate([base[:, :, 0:1, :], paired, base[:, :, 2:3, :]], axis=2)
    scaled = jnp.clip(base * D ** (-0.5), -0.6, 0.6)
    return scaled.reshape(D, 3 * HEADS * HEAD_DIM).astype(jnp.bfloat16)


def draw_gains_space(key, part):
    key = jax.random.fold_in(key, 5)
    return gain_draw(key, 0.5, 2.0)


def draw_gains_time(key, part):
    key = jax.random.fold_in(key, 7)
    return gain_draw(key, 0.5, 2.0)


def draw_qkv_space(key, part):
    key = jax.random.fold_in(key, 11)
    return qkv_draw(key)


def draw_qkv_time(key, part):
    key = jax.random.fold_in(key, 13)
    return qkv_draw(key)


def levels(rng, dims, cuts, least, largest):
    level, own = 1.0, jax.random.fold_in(rng, 6)
    for position, shards_of in cuts:
        steps = jnp.exp(jax.random.uniform(jax.random.fold_in(own, position), (shards_of,), jnp.float32, least / len(cuts), largest / len(cuts)))
        level = level * jnp.repeat(steps, dims[position] // shards_of).reshape([-1 if axis == position else 1 for axis in range(len(dims))])
    return level


def normal_values(rng, dims, scale, bound, shards=(), held_as=jnp.bfloat16):
    array = jax.random.normal(rng, dims, jnp.float32) * scale
    if len(shards) > 0:
        array = levels(rng, dims, shards, -0.22, 0.18) * array
    return jnp.clip(array, min=-bound, max=bound).astype(held_as)


def setup_inputs(seed: int = 0) -> dict:
    splits = jax.random.split(jax.random.key(seed), 12)
    return {
        "tokens": normal_values(splits[0], (VIDEOS, FRAMES, PATCHES, D), 1.0, 6.0, ((0, 2), (1, 16), (2, 8))),
        "validity": draw_validity(jax.random.fold_in(splits[11], 71), 0),
        "table_space": normal_values(splits[2], (3, D), 0.7, 3.0, (), jnp.float32),
        "qkv_space": draw_qkv_space(jax.random.fold_in(splits[11], 71), 0),
        "gains_space": draw_gains_space(jax.random.fold_in(splits[11], 71), 0),
        "out_space": normal_values(splits[5], (HEADS * HEAD_DIM, D), (HEADS * HEAD_DIM) ** -0.5, 0.25),
        "table_time": normal_values(splits[6], (3, D), 0.7, 3.0, (), jnp.float32),
        "qkv_time": draw_qkv_time(jax.random.fold_in(splits[11], 71), 0),
        "gains_time": draw_gains_time(jax.random.fold_in(splits[11], 71), 0),
        "out_time": normal_values(splits[9], (HEADS * HEAD_DIM, D), (HEADS * HEAD_DIM) ** -0.5, 0.25),
        "cotangent": normal_values(splits[10], (VIDEOS, FRAMES, PATCHES, D), 1.0, 6.0, ((0, 2), (1, 16), (2, 8))),
    }


EPSILON = 1e-06

def modulate(inputs, mod_table):
    values = inputs.astype(jnp.float32)
    centred = values - lax.optimization_barrier(jnp.mean(values, axis=-1, keepdims=True))
    inv_std = lax.rsqrt(lax.optimization_barrier(jnp.mean(centred * centred, axis=-1, keepdims=True)) + EPSILON)
    normed = centred * inv_std
    shifted = (normed * (1.0 + mod_table[1]) + mod_table[0]).astype(jnp.bfloat16)
    return (normed, inv_std, shifted)

def modulate_back(grad_mod, normed, inv_std, mod_table):
    grad_norm = grad_mod * (1.0 + mod_table[1])
    grad_in = inv_std * (grad_norm - lax.optimization_barrier(jnp.mean(grad_norm, axis=-1, keepdims=True)) - normed * lax.optimization_barrier(jnp.mean(grad_norm * normed, axis=-1, keepdims=True)))
    feature_dim = grad_mod.shape[-1]
    grad_shift = lax.optimization_barrier(jnp.sum(grad_mod.reshape(-1, feature_dim), axis=0))
    grad_scale = lax.optimization_barrier(jnp.sum((grad_mod * normed).reshape(-1, feature_dim), axis=0))
    return (grad_in, grad_shift, grad_scale)

def rms_scale(raw_vals):
    return lax.rsqrt(lax.optimization_barrier(jnp.mean(raw_vals * raw_vals, axis=-1, keepdims=True)) + EPSILON)

def rms_back(grad_vals, raw_vals, inv_vals):
    return inv_vals * (grad_vals - raw_vals * inv_vals * inv_vals * lax.optimization_barrier(jnp.mean(grad_vals * raw_vals, axis=-1, keepdims=True)))

def project(shifted, weight_qkv, qk_gains):
    head_dim = qk_gains.shape[1]
    head_count = weight_qkv.shape[1] // (3 * head_dim)
    rows_in = shifted.reshape(-1, shifted.shape[-1])
    raw_proj = jnp.dot(rows_in, weight_qkv, preferred_element_type=jnp.float32)
    raw_proj = raw_proj.reshape(shifted.shape[:-1] + (head_count, 3, head_dim))
    query_raw = raw_proj[..., 0, :]
    key_raw = raw_proj[..., 1, :]
    query_inv = rms_scale(query_raw)
    key_inv = rms_scale(key_raw)
    stacked = jnp.stack([query_raw * query_inv * qk_gains[0], key_raw * key_inv * qk_gains[1], raw_proj[..., 2, :]], axis=-2)
    return (stacked.astype(jnp.bfloat16), (query_raw, query_inv, key_raw, key_inv))

def project_back(grad_qkv, saved, weight_qkv, qk_gains):
    query_raw, query_inv, key_raw, key_inv = saved
    grad_query = rms_back(grad_qkv[..., 0, :].astype(jnp.float32) * qk_gains[0], query_raw, query_inv)
    grad_key = rms_back(grad_qkv[..., 1, :].astype(jnp.float32) * qk_gains[1], key_raw, key_inv)
    grad_value = grad_qkv[..., 2, :].astype(jnp.float32)
    grad_raw = jnp.stack([grad_query, grad_key, grad_value], axis=-2).astype(jnp.bfloat16)
    leading = grad_raw.shape[:-3]
    grad_rows = grad_raw.reshape(-1, weight_qkv.shape[1])
    grad_shifted = jnp.dot(grad_rows, weight_qkv.T, preferred_element_type=jnp.float32)
    return grad_shifted.reshape(leading + (weight_qkv.shape[0],))

def finish(inputs, attended, mod_table, weight_out, token_mask):
    branch = jnp.dot(attended.reshape(-1, attended.shape[-1]), weight_out, preferred_element_type=jnp.float32)
    branch = branch.reshape(inputs.shape)
    result = (inputs.astype(jnp.float32) + token_mask * mod_table[2] * branch).astype(jnp.bfloat16)
    return (result, branch)

def finish_back(grad_res, attended, branch, mod_table, weight_out, token_mask):
    masked = grad_res * token_mask
    feature_dim = masked.shape[-1]
    grad_gate = lax.optimization_barrier(jnp.sum((masked * branch).reshape(-1, feature_dim), axis=0))
    grad_branch = (masked * mod_table[2]).astype(jnp.bfloat16).reshape(-1, feature_dim)
    grad_att = jnp.dot(grad_branch, weight_out.T, preferred_element_type=jnp.float32)
    return (grad_att.astype(jnp.bfloat16).reshape(attended.shape), grad_branch, grad_gate)

def seq_forward(sequence, key_mask):
    head_dim = sequence.shape[-1]
    queries = sequence[:, 0]
    keys_in = sequence[:, 1]
    values = sequence[:, 2]
    scores = jnp.dot(queries, keys_in.T, preferred_element_type=jnp.float32) * head_dim ** (-0.5)
    scores = jnp.where(key_mask[None, :] > 0.5, scores, jnp.float32(-1e+30))
    highest = lax.optimization_barrier(jnp.max(scores, axis=-1, keepdims=True))
    weights_exp = jnp.exp(scores - highest)
    attn_weights = weights_exp / lax.optimization_barrier(jnp.sum(weights_exp, axis=-1, keepdims=True))
    output = jnp.dot(attn_weights.astype(jnp.bfloat16), values, preferred_element_type=jnp.float32)
    return (output.astype(jnp.bfloat16), attn_weights)

def seq_backward(sequence, key_mask, grad_output):
    head_dim = sequence.shape[-1]
    queries = sequence[:, 0]
    keys_in = sequence[:, 1]
    values = sequence[:, 2]
    attn_weights = seq_forward(sequence, key_mask)[1]
    rounded = attn_weights.astype(jnp.bfloat16)
    grad_values = jnp.dot(rounded.T, grad_output, preferred_element_type=jnp.float32)
    grad_weights = jnp.dot(grad_output, values.T, preferred_element_type=jnp.float32)
    grad_scores = attn_weights * (grad_weights - lax.optimization_barrier(jnp.sum(grad_weights * attn_weights, axis=-1, keepdims=True))) * head_dim ** (-0.5)
    grad_round = grad_scores.astype(jnp.bfloat16)
    grad_queries = jnp.dot(grad_round, keys_in, preferred_element_type=jnp.float32)
    grad_keys = jnp.dot(grad_round.T, queries, preferred_element_type=jnp.float32)
    return jnp.stack([grad_queries, grad_keys, grad_values], axis=1).astype(jnp.bfloat16)

def run_core(packed, key_mask):
    seq_count, length, head_count, _, head_dim = packed.shape
    sequences = jnp.moveaxis(packed, 2, 1).reshape(seq_count * head_count, length, 3, head_dim)

    def single(sequence):
        return seq_forward(sequence, key_mask)[0]
    if length >= 512:
        outputs = lax.map(single, sequences)
    else:
        outputs = jax.vmap(single)(sequences)
    return jnp.moveaxis(outputs.reshape(seq_count, head_count, length, head_dim), 1, 2)

def run_core_back(packed, key_mask, grad_out):
    seq_count, length, head_count, _, head_dim = packed.shape
    sequences = jnp.moveaxis(packed, 2, 1).reshape(seq_count * head_count, length, 3, head_dim)
    grad_seqs = jnp.moveaxis(grad_out, 2, 1).reshape(seq_count * head_count, length, head_dim)

    def single(pair):
        return seq_backward(pair[0], key_mask, pair[1])
    if length >= 512:
        grads = lax.map(single, (sequences, grad_seqs))
    else:
        grads = jax.vmap(single)((sequences, grad_seqs))
    return jnp.moveaxis(grads.reshape(seq_count, head_count, length, 3, head_dim), 1, 2)

def reference(tokens, validity, table_space, qkv_space, gains_space, out_space, table_time, qkv_time, gains_time, out_time, cotangent):
    video_count, frame_count, patch_count, feature_dim = tokens.shape
    head_dim = gains_space.shape[1]
    head_count = qkv_space.shape[1] // (3 * head_dim)
    key_mask = validity.astype(jnp.float32)
    token_mask = key_mask[None, None, :, None]
    time_mask = jnp.ones((frame_count,), jnp.float32)
    normed_s, inv_s, shifted_s = modulate(tokens, table_space)
    packed_s, saved_s = project(shifted_s, qkv_space, gains_space)
    seq_space = packed_s.reshape(video_count * frame_count, patch_count, head_count, 3, head_dim)
    attended_s = run_core(seq_space, key_mask).reshape(video_count, frame_count, patch_count, head_count * head_dim)
    middle, branch_s = finish(tokens, attended_s, table_space, out_space, token_mask)
    normed_t, inv_t, shifted_t = modulate(middle, table_time)
    packed_t, saved_t = project(shifted_t, qkv_time, gains_time)
    seq_time = packed_t.reshape(video_count, frame_count, patch_count * head_count, 3, head_dim)
    attended_t = run_core(seq_time, time_mask).reshape(video_count, frame_count, patch_count, head_count * head_dim)
    mixed, branch_t = finish(middle, attended_t, table_time, out_time, token_mask)
    grad_res = cotangent.astype(jnp.float32)
    grad_att_t, grad_branch_t, gate_time = finish_back(grad_res, attended_t, branch_t, table_time, out_time, token_mask)
    grad_out_time = jnp.dot(attended_t.reshape(-1, head_count * head_dim).T, grad_branch_t, preferred_element_type=jnp.float32)
    grad_seq_t = run_core_back(seq_time, time_mask, grad_att_t.reshape(video_count, frame_count, patch_count * head_count, head_dim))
    grad_shift_t = project_back(grad_seq_t.reshape(packed_t.shape), saved_t, qkv_time, gains_time)
    grad_in_t, shift_time, scale_time = modulate_back(grad_shift_t, normed_t, inv_t, table_time)
    grad_middle = (grad_res + grad_in_t).astype(jnp.bfloat16)
    grad_mid = lax.optimization_barrier(grad_middle).astype(jnp.float32)
    grad_att_s, grad_branch_s, gate_space = finish_back(grad_mid, attended_s, branch_s, table_space, out_space, token_mask)
    grad_out_space = jnp.dot(attended_s.reshape(-1, head_count * head_dim).T, grad_branch_s, preferred_element_type=jnp.float32)
    grad_seq_s = run_core_back(seq_space, key_mask, grad_att_s.reshape(video_count * frame_count, patch_count, head_count, head_dim))
    grad_shift_s = project_back(grad_seq_s.reshape(packed_s.shape), saved_s, qkv_space, gains_space)
    grad_in_s, shift_space, scale_space = modulate_back(grad_shift_s, normed_s, inv_s, table_space)
    token_grad = (grad_mid + grad_in_s).astype(jnp.bfloat16)
    grad_tables = jnp.stack([jnp.stack([shift_space, scale_space, gate_space]), jnp.stack([shift_time, scale_time, gate_time])])
    return (mixed, token_grad, grad_out_space, grad_out_time, grad_tables)
```

```python
import functools

import jax
import jax.numpy as jnp
from jax import lax
from jax.experimental import pallas as pl
from jax.experimental.pallas import tpu as pltpu
from jax.sharding import PartitionSpec as P

MESH = pl.DeviceIdType.MESH
BF = jnp.bfloat16
F32 = jnp.float32
EPSILON = 1e-6

NN = (((1,), (0,)), ((), ()))
NT = (((1,), (1,)), ((), ()))
TN = (((0,), (0,)), ((), ()))


def dot(a, b, dims=NN):
    return lax.dot_general(a, b, dims, preferred_element_type=F32)


def mean(v):
    return jnp.mean(v, axis=-1, keepdims=True)


def norm(values):
    centred = values - mean(values)
    inv_std = lax.rsqrt(mean(centred * centred) + EPSILON)
    return centred * inv_std, inv_std


def rms_scale(raw):
    return lax.rsqrt(mean(raw * raw) + EPSILON)


def rms_back(grad, raw):
    inv = rms_scale(raw)
    return inv * (grad - raw * (inv * inv) * mean(grad * raw))


def modulate_back(grad, normed, inv_std, table):
    grad_norm = grad * (1.0 + table[1:2, :])
    grad_in = inv_std * (grad_norm - mean(grad_norm) - normed * mean(grad_norm * normed))
    shift = jnp.sum(grad, axis=0, keepdims=True)
    scale = jnp.sum(grad * normed, axis=0, keepdims=True)
    return grad_in, shift, scale


class Sizes:
    pass


def to_blocks(rows, cut):
    n, width = rows.shape[0] // 8, rows.shape[1]
    cube = rows.reshape(n, 8, width)
    low = jnp.concatenate([cube[:, :, cut:], jnp.zeros((n, 8, 2 * cut - width), F32)], axis=2)
    return jnp.concatenate([cube[:, :, :cut], low], axis=1).astype(BF)


def from_blocks(blocks, width):
    n, _, cut = blocks.shape
    cube = blocks.astype(F32)
    full = jnp.concatenate([cube[:, :8, :], cube[:, 8:, : width - cut]], axis=2)
    return full.reshape(n * 8, width)


def to_lines(rows, lines):
    third = rows[0].shape[1] // 3
    parts = [r[:, third * c : third * (c + 1)] for r in rows for c in range(3)]
    if lines > len(parts):
        parts.append(jnp.zeros((lines - len(parts), third), F32))
    return jnp.concatenate(parts, axis=0)


def from_lines(lines, r):
    return jnp.concatenate([lines[3 * r + c : 3 * r + c + 1, :] for c in range(3)], axis=1)


def kernel(z, names, *refs):
    r = Sizes()
    for name, ref in zip(names, refs):
        setattr(r, name, ref)
    heads, hd, width, toks, ns, nt, nz, cut = (
        z.heads, z.hd, z.width, z.toks, z.ns, z.nt, z.nz, z.cut,
    )
    att_w = heads * hd
    scaling = hd ** (-0.5)
    dp = lax.axis_index("dp")
    tm = lax.axis_index("tm")
    sp = lax.axis_index("space")
    core, y = sp % 2, sp // 2
    x_lo, zz = tm // nz, tm % nz
    x = dp * 2 + x_lo
    nx = 4
    ny = ns // 2

    def remote(src, dst, send_sem, recv_sem, device):
        return pltpu.make_async_remote_copy(
            src_ref=src, dst_ref=dst, send_sem=send_sem, recv_sem=recv_sem,
            device_id=device, device_id_type=MESH,
        )

    groups = {
        "space": (ns, sp, lambda j: (dp, tm, j)),
        "tm": (nt, tm, lambda j: (dp, j, sp)),
        "y": (ny, y, lambda j: (dp, tm, j * 2 + core)),
        "x": (nx, x, lambda j: (j // 2, (j % 2) * nz + zz, sp)),
        "z": (nz, zz, lambda j: (dp, x_lo * nz + j, sp)),
    }

    def exchange(group, src_of, recv, sems, d):
        n, me, device = groups[group]
        j = (me + d) % n
        return remote(src_of(j), recv.at[me], sems.at[0, d], sems.at[1, me], device(j))

    def start_all(group, src_of, recv, sems):
        n = groups[group][0]

        def body(d, carry):
            exchange(group, src_of, recv, sems, d).start()
            return carry

        lax.fori_loop(1, n, body, 0)

    def wait_from(group, src_of, recv, sems, j):
        n, me, device = groups[group]
        remote(src_of(j), recv.at[j], sems.at[0, 0], sems.at[1, j], device(j)).wait_recv()

    def wait_all(group, src_of, recv, sems):
        n, me, _ = groups[group]

        def body(d, carry):
            wait_from(group, src_of, recv, sems, (me + d) % n)
            return carry

        lax.fori_loop(1, n, body, 0)

    def wait_sent(group, src_of, recv, sems):
        n = groups[group][0]

        def body(d, carry):
            exchange(group, src_of, recv, sems, d).wait_send()
            return carry

        lax.fori_loop(1, n, body, 0)

    weight_copies = [
        pltpu.make_async_copy(src, dst, r.w_sem.at[i])
        for i, (src, dst) in enumerate(
            [(r.qkv_s, r.wqs), (r.out_s, r.wos), (r.qkv_t, r.wqt), (r.out_t, r.wot)]
        )
    ]
    for copy in weight_copies:
        copy.start()
    barrier = pltpu.get_barrier_semaphore()

    def signal(device):
        pl.semaphore_signal(barrier, inc=1, device_id=device, device_id_type=MESH)

    def greet(group):
        n, me, device = groups[group]

        def body(d, carry):
            signal(device((me + d) % n))
            return carry

        lax.fori_loop(1, n, body, 0)

    greet("space")
    greet("tm")
    other = 1 - dp
    signal((other, tm, sp))
    signal((other, (1 - x_lo) * nz + zz, sp))

    val = r.val[...].astype(F32)
    key_row = jnp.concatenate([val[j : j + 1, :] for j in range(ns)], axis=1)
    own_row = r.val[pl.ds(sp, 1), :].astype(F32)
    row_id = lax.broadcasted_iota(jnp.int32, (toks, toks), 0)
    col_id = lax.broadcasted_iota(jnp.int32, (toks, toks), 1)
    own = jnp.broadcast_to(own_row, (toks, toks))
    mask_s = jnp.sum(jnp.where(row_id == col_id, own, 0.0), axis=1, keepdims=True)
    mask_t = jnp.sum(jnp.where(tm * 8 + row_id % 8 == col_id, own, 0.0), axis=1, keepdims=True)

    def project(shifted, weight, gains, raw_ref, emit):
        raw_ref[...] = dot(shifted, weight)
        g = gains[...]
        for h in range(heads):
            base = 3 * hd * h
            p0 = raw_ref[:, base : base + hd]
            p1 = raw_ref[:, base + hd : base + 2 * hd]
            p2 = raw_ref[:, base + 2 * hd : base + 3 * hd]
            emit(h, p0 * rms_scale(p0) * g[0:1, :], p1 * rms_scale(p1) * g[1:2, :], p2)

    def project_back(h, dq, dk, dv, raw_ref, gains):
        g = gains[...]
        base = 3 * hd * h
        p0 = raw_ref[:, base : base + hd]
        p1 = raw_ref[:, base + hd : base + 2 * hd]
        r.grw[:, base : base + hd] = rms_back(dq * g[0:1, :], p0)
        r.grw[:, base + hd : base + 2 * hd] = rms_back(dk * g[1:2, :], p1)
        r.grw[:, base + 2 * hd : base + 3 * hd] = dv

    tokens = r.tok[...].astype(F32)
    table_s = r.tab_s[...]
    normed, _ = norm(tokens)
    shifted = (normed * (1.0 + table_s[1:2, :]) + table_s[0:1, :]).astype(BF)
    r.cot_send[...] = to_blocks(r.cot[...].astype(F32), cut)
    r.cot_recv[tm] = r.cot_send[tm]

    weight_copies[0].wait()

    def emit_s(h, q, k, v):
        packed = jnp.concatenate([q, k, v, jnp.zeros((toks, 256 - 3 * hd), F32)], axis=1)
        r.ps_send[h] = packed.astype(BF)

    project(shifted, r.wqs[...], r.gn_s, r.raw_s, emit_s)
    r.ps_recv[sp] = r.ps_send[sp]

    pl.semaphore_wait(barrier, ns - 1 + nt - 1 + 2)
    ps = ("space", lambda j: r.ps_send.at[j], r.ps_recv, r.ps_sem)
    start_all(*ps)
    ct = ("tm", lambda j: r.cot_send.at[j], r.cot_recv, r.cot_sem)
    start_all(*ct)
    wait_all(*ps)

    for j in range(ns):
        block = r.ps_recv[j].astype(F32)
        r.q_ref[j] = block[:, :hd].astype(BF)
        r.k_ref[toks * j : toks * (j + 1), :] = block[:, hd : 2 * hd].astype(BF)
        r.v_ref[toks * j : toks * (j + 1), :] = block[:, 2 * hd : 3 * hd].astype(BF)

    at = ("space", lambda j: r.at_send.at[j], r.at_recv, r.at_sem)

    def attend(d, carry):
        j = (sp + d) % ns
        scores = dot(r.q_ref[j], r.k_ref[...], NT) * scaling
        scores = jnp.where(key_row > 0.5, scores, -1e30)
        exps = jnp.exp(scores - jnp.max(scores, axis=-1, keepdims=True))
        weights = exps * (1.0 / jnp.sum(exps, axis=-1, keepdims=True))
        r.prob[j] = weights
        r.at_send[j] = dot(weights.astype(BF), r.v_ref[...]).astype(BF)

        @pl.when(d < ns)
        def _():
            exchange(*at, d).start()

        return carry

    lax.fori_loop(1, ns + 1, attend, 0)
    r.at_recv[sp] = r.at_send[sp]
    wait_all(*at)
    for h in range(heads):
        r.att_f[:, hd * h : hd * (h + 1)] = r.at_recv[h].astype(F32)
    r.att_s[...] = r.att_f[...].astype(BF)
    weight_copies[1].wait()
    branch_s = dot(r.att_s[...], r.wos[...])
    r.branch_s[...] = branch_s
    middle = r.tok[...].astype(F32) + mask_s * table_s[2:3, :] * branch_s
    r.mid_send[...] = to_blocks(middle, cut)
    r.mid_recv[tm] = r.mid_send[tm]
    md = ("tm", lambda j: r.mid_send.at[j], r.mid_recv, r.mid_sem)
    start_all(*md)

    table_t = r.tab_t[...]
    wait_all(*ct)
    cot = from_blocks(r.cot_recv[...], width)
    masked = cot * mask_t
    grad_branch = (masked * table_t[2:3, :]).astype(BF)
    r.gb_t[...] = grad_branch
    weight_copies[3].wait()
    r.grad_att[...] = dot(grad_branch, r.wot[...], NT)

    wait_all(*md)
    middle = from_blocks(r.mid_recv[...], width)
    normed, inv_t = norm(middle)
    shifted = (normed * (1.0 + table_t[1:2, :]) + table_t[0:1, :]).astype(BF)
    weight_copies[2].wait()
    same = row_id % 8 == col_id % 8

    def emit_t(h, q, k, v):
        q, k, v = q.astype(BF), k.astype(BF), v.astype(BF)
        scores = jnp.where(same, dot(q, k, NT) * scaling, -1e30)
        exps = jnp.exp(scores - jnp.max(scores, axis=-1, keepdims=True))
        weights = exps * (1.0 / jnp.sum(exps, axis=-1, keepdims=True))
        rounded = weights.astype(BF)
        r.att_f[:, hd * h : hd * (h + 1)] = dot(rounded, v)
        grad_out = r.grad_att[:, hd * h : hd * (h + 1)].astype(BF)
        dv = dot(rounded, grad_out, TN)
        dw = dot(grad_out, v, NT)
        ds = weights * (dw - jnp.sum(dw * weights, axis=-1, keepdims=True)) * scaling
        ds = ds.astype(BF)
        dq = dot(ds, k)
        dk = dot(ds, q, TN)
        project_back(
            h,
            dq.astype(BF).astype(F32),
            dk.astype(BF).astype(F32),
            dv.astype(BF).astype(F32),
            r.raw_t,
            r.gn_t,
        )

    project(shifted, r.wqt[...], r.gn_t, r.raw_t, emit_t)
    grad_shifted = dot(r.grw[...].astype(BF), r.wqt[...], NT)
    normed, inv_t = norm(from_blocks(r.mid_recv[...], width))
    grad_in, shift_t, scale_t = modulate_back(grad_shifted, normed, inv_t, table_t)
    cot = from_blocks(r.cot_recv[...], width)
    r.gm_send[...] = to_blocks(cot + grad_in, cut)
    r.gm_recv[tm] = r.gm_send[tm]
    gm = ("tm", lambda j: r.gm_send.at[j], r.gm_recv, r.gm_sem)
    start_all(*gm)

    att_t = r.att_f[...].astype(BF)
    branch_t = dot(att_t, r.wot[...])
    middle = from_blocks(r.mid_recv[...], width)
    r.mix_send[...] = to_blocks(middle + mask_t * table_t[2:3, :] * branch_t, cut)
    r.mix_recv[tm] = r.mix_send[tm]
    mx = ("tm", lambda j: r.mix_send.at[j], r.mix_recv, r.mix_sem)
    start_all(*mx)
    gate_t = jnp.sum(from_blocks(r.cot_recv[...], width) * mask_t * branch_t, axis=0, keepdims=True)

    pair = (dp, tm, sp + 1 - 2 * core)

    def pair_copy(a):
        return remote(
            r.part.at[a, 1 - core], r.pair_recv.at[a], r.pair_sem.at[0, a], r.pair_sem.at[1, a], pair
        )

    def partial_grad(a, att, grad_branch):
        full = dot(att, grad_branch, TN)
        pad = jnp.zeros((z.rows - hd, width), F32)
        for h in range(heads):
            block = jnp.concatenate([full[hd * h : hd * (h + 1), :], pad], axis=0)
            r.part[a, h % 2, h // 2] = block.astype(BF)
        pair_copy(a).start()

    def rs_args(kind, a):
        send, recv, sems = {
            "y": (r.y_send, r.y_recv, r.y_sem),
            "x": (r.x_send, r.x_recv, r.x_sem),
            "z": (r.z_send, r.z_recv, r.z_sem),
        }[kind]
        return (kind, lambda j: send.at[a, j], recv.at[a], sems.at[a])

    def rs_y(a):
        pair_copy(a).wait_recv()
        r.y_send[a] = (r.part[a, core].astype(F32) + r.pair_recv[a].astype(F32)).astype(BF)
        r.y_recv[a, y] = r.y_send[a, y]
        start_all(*rs_args("y", a))

    def total(ref, a, n):
        value = ref[a, 0].astype(F32)
        for j in range(1, n):
            value = value + ref[a, j].astype(F32)
        return value

    def rs_x(a):
        wait_all(*rs_args("y", a))
        value = total(r.y_recv, a, ny)
        part_w = width // nx
        for j in range(nx):
            r.x_send[a, j] = value[:, part_w * j : part_w * (j + 1)].astype(BF)
        r.x_recv[a, x] = r.x_send[a, x]
        start_all(*rs_args("x", a))

    def rs_z(a):
        wait_all(*rs_args("x", a))
        value = total(r.x_recv, a, nx)
        part_w = width // nx // nz
        for j in range(nz):
            r.z_send[a, j] = value[:, part_w * j : part_w * (j + 1)].astype(BF)
        r.z_recv[a, zz] = r.z_send[a, zz]
        start_all(*rs_args("z", a))

    def rs_end(a, out_ref):
        wait_all(*rs_args("z", a))
        out_ref[...] = total(r.z_recv, a, nz)[:hd, :]

    partial_grad(0, att_t, r.gb_t[...])
    rs_y(0)

    wait_all(*gm)
    grad_mid = from_blocks(r.gm_recv[...], width)
    r.grad_mid[...] = grad_mid
    masked = grad_mid * mask_s
    grad_branch = (masked * table_s[2:3, :]).astype(BF)
    r.gb_s[...] = grad_branch
    grad_att = dot(grad_branch, r.wos[...], NT)
    for h in range(heads):
        r.do_send[h] = grad_att[:, hd * h : hd * (h + 1)].astype(BF)
    r.do_recv[sp] = r.do_send[sp]
    do = ("space", lambda j: r.do_send.at[j], r.do_recv, r.do_sem)
    start_all(*do)
    gate_s = jnp.sum(r.grad_mid[...] * mask_s * r.branch_s[...], axis=0, keepdims=True)
    partial_grad(1, r.att_s[...], r.gb_s[...])

    def table_args(kind, k):
        send, recv, sems = getattr(r, k + kind + "_send"), getattr(r, k + kind + "_recv"), getattr(r, k + kind + "_sem")
        return (kind if kind != "s" else "space", lambda j: send, recv, sems)

    def table_start(kind, k, value):
        args = table_args(kind, k)
        getattr(r, k + kind + "_send")[...] = value
        args[2][groups[args[0]][1]] = value
        start_all(*args)

    def table_sum(kind, k):
        args = table_args(kind, k)
        wait_all(*args)
        value = args[2][0]
        for j in range(1, groups[args[0]][0]):
            value = value + args[2][j]
        return value

    r.dk_t[...] = jnp.zeros_like(r.dk_t)
    r.dv_t[...] = jnp.zeros_like(r.dv_t)

    def attend_back(d, carry):
        j = (sp + d) % ns

        @pl.when(d > 0)
        def _():
            wait_from(*do, j)

        weights = r.prob[j]
        grad_out = r.do_recv[j]
        dw = dot(grad_out, r.v_ref[...], NT)
        ds = weights * (dw - jnp.sum(dw * weights, axis=-1, keepdims=True)) * scaling
        ds = ds.astype(BF)
        r.dq[j] = dot(ds, r.k_ref[...])
        r.dv_t[...] += dot(grad_out, weights.astype(BF), TN)
        r.dk_t[...] += dot(r.q_ref[j], ds, TN)
        return carry

    lax.fori_loop(0, ns, attend_back, 0)
    for j in range(ns):
        dk = r.dk_t[:, toks * j : toks * (j + 1)].T
        dv = r.dv_t[:, toks * j : toks * (j + 1)].T
        packed = jnp.concatenate(
            [r.dq[j], dk, dv, jnp.zeros((toks, 256 - 3 * hd), F32)], axis=1
        )
        r.gp_send[j] = packed.astype(BF)
    r.gp_recv[sp] = r.gp_send[sp]
    gp = ("space", lambda j: r.gp_send.at[j], r.gp_recv, r.gp_sem)
    start_all(*gp)

    rs_y(1)
    rs_x(0)
    table_start("s", "e", to_lines([shift_t, scale_t, gate_t, gate_s], 16))
    wait_all(*mx)
    r.mixed[...] = from_blocks(r.mix_recv[...], width).astype(BF)

    wait_all(*gp)
    for h in range(heads):
        block = r.gp_recv[h].astype(F32)
        project_back(
            h, block[:, :hd], block[:, hd : 2 * hd], block[:, 2 * hd : 3 * hd], r.raw_s, r.gn_s
        )
    grad_shifted = dot(r.grw[...].astype(BF), r.wqs[...], NT)
    normed, inv_s = norm(r.tok[...].astype(F32))
    grad_in, shift_s, scale_s = modulate_back(grad_shifted, normed, inv_s, table_s)
    table_start("s", "l", to_lines([shift_s, scale_s], 8))
    r.tgrad[...] = (r.grad_mid[...] + grad_in).astype(BF)
    rs_x(1)
    rs_z(0)
    table_start("x", "e", table_sum("s", "e"))
    table_start("x", "l", table_sum("s", "l"))
    rs_z(1)
    table_start("z", "e", table_sum("x", "e"))
    table_start("z", "l", table_sum("x", "l"))
    rs_end(0, r.got)
    rs_end(1, r.gos)
    early = table_sum("z", "e")
    late = table_sum("z", "l")
    rows = [from_lines(late, 0), from_lines(late, 1), from_lines(early, 3)]
    rows += [from_lines(early, 0), from_lines(early, 1), from_lines(early, 2)]
    for i in range(6):
        r.tabs[i : i + 1, :] = rows[i]

    for args in (ps, ct, at, md, gm, mx, do, gp):
        wait_sent(*args)
    for a in range(2):
        pair_copy(a).wait_send()
        for kind in ("y", "x", "z"):
            wait_sent(*rs_args(kind, a))
    for k in ("e", "l"):
        for kind in ("s", "x", "z"):
            wait_sent(*table_args(kind, k))


def solution(mesh):
    nt, ns = mesh.shape["tm"], mesh.shape["space"]

    def on_device(
        tokens, validity, table_space, qkv_space, gains_space, out_space,
        table_time, qkv_time, gains_time, out_time, cotangent,
    ):
        z = Sizes()
        z.width = tokens.shape[3]
        z.toks = tokens.shape[2]
        z.hd = gains_space.shape[1]
        z.heads = out_space.shape[0] // z.hd
        z.ns, z.nt, z.nz = ns, nt, nt // 2
        z.cut = 640
        z.rows = 80
        heads, hd, width, toks, nz = z.heads, z.hd, z.width, z.toks, z.nz
        qw = 3 * heads * hd
        dma = pltpu.SemaphoreType.DMA
        vm = pltpu.VMEM
        third = width // 3
        scratch = {
            "wqs": vm((width, qw), BF),
            "wos": vm((heads * hd, width), BF),
            "wqt": vm((width, qw), BF),
            "wot": vm((heads * hd, width), BF),
            "w_sem": dma((4,)),
            "raw_s": vm((toks, qw), F32),
            "raw_t": vm((toks, qw), F32),
            "grw": vm((toks, qw), F32),
            "q_ref": vm((ns, toks, hd), BF),
            "k_ref": vm((ns * toks, hd), BF),
            "v_ref": vm((ns * toks, hd), BF),
            "prob": vm((ns, toks, ns * toks), F32),
            "dq": vm((ns, toks, hd), F32),
            "dk_t": vm((hd, ns * toks), F32),
            "dv_t": vm((hd, ns * toks), F32),
            "att_f": vm((toks, heads * hd), F32),
            "att_s": vm((toks, heads * hd), BF),
            "branch_s": vm((toks, width), F32),
            "grad_att": vm((toks, heads * hd), F32),
            "grad_mid": vm((toks, width), F32),
            "gb_t": vm((toks, width), BF),
            "gb_s": vm((toks, width), BF),
            "part": vm((2, 2, ns // 2, z.rows, width), BF),
            "pair_recv": vm((2, ns // 2, z.rows, width), BF),
            "pair_sem": dma((2, 2)),
        }

        def both(name, n, shape, dtype):
            scratch[name + "_send"] = vm((n,) + shape, dtype)
            scratch[name + "_recv"] = vm((n,) + shape, dtype)
            scratch[name + "_sem"] = dma((2, n))

        both("ps", ns, (toks, 256), BF)
        both("gp", ns, (toks, 256), BF)
        both("at", ns, (toks, hd), BF)
        both("do", ns, (toks, hd), BF)
        for name in ("cot", "mid", "gm", "mix"):
            both(name, nt, (16, z.cut), BF)
        for name, n, w in (("y", ns // 2, width), ("x", 4, width // 4), ("z", nz, width // 4 // nz)):
            scratch[name + "_send"] = vm((2, n, z.rows, w), BF)
            scratch[name + "_recv"] = vm((2, n, z.rows, w), BF)
            scratch[name + "_sem"] = dma((2, 2, n))
        for k, lines in (("e", 16), ("l", 8)):
            for kind, n in (("s", ns), ("x", 4), ("z", nz)):
                scratch[k + kind + "_send"] = vm((lines, third), F32)
                scratch[k + kind + "_recv"] = vm((n, lines, third), F32)
                scratch[k + kind + "_sem"] = dma((2, n))

        ins = ["tok", "cot", "val", "tab_s", "gn_s", "tab_t", "gn_t", "qkv_s", "out_s", "qkv_t", "out_t"]
        outs = ["mixed", "tgrad", "gos", "got", "tabs"]
        vmem = pl.BlockSpec(memory_space=pltpu.VMEM)
        anywhere = pl.BlockSpec(memory_space=pl.ANY)
        mixed, tgrad, gos, got, tabs = pl.pallas_call(
            functools.partial(kernel, z, ins + outs + list(scratch)),
            out_shape=[
                jax.ShapeDtypeStruct((toks, width), BF),
                jax.ShapeDtypeStruct((toks, width), BF),
                jax.ShapeDtypeStruct((hd, width // 4 // nz), F32),
                jax.ShapeDtypeStruct((hd, width // 4 // nz), F32),
                jax.ShapeDtypeStruct((6, width), F32),
            ],
            in_specs=[vmem] * 7 + [anywhere] * 4,
            out_specs=[vmem] * 5,
            scratch_shapes=list(scratch.values()),
            compiler_params=pltpu.CompilerParams(
                collective_id=0, has_side_effects=True, vmem_limit_bytes=56 * 1024 * 1024
            ),
        )(
            tokens.reshape(toks, width),
            cotangent.reshape(toks, width),
            validity.reshape(ns, toks),
            table_space,
            gains_space,
            table_time,
            gains_time,
            qkv_space,
            out_space,
            qkv_time,
            out_time,
        )
        shape = tokens.shape
        return mixed.reshape(shape), tgrad.reshape(shape), gos, got, tabs.reshape(2, 3, width)

    spread = P("dp", "tm", "space", None)
    return jax.shard_map(
        on_device,
        mesh=mesh,
        in_specs=(spread,) + (P(),) * 9 + (spread,),
        out_specs=(spread, spread, P("space", ("dp", "tm")), P("space", ("dp", "tm")), P()),
        check_vma=False,
    )
```

```python
import functools

import jax
import jax.numpy as jnp
from jax import lax
from jax.experimental import pallas as pl
from jax.experimental.pallas import tpu as pltpu
from jax.sharding import PartitionSpec as P

MESH = pl.DeviceIdType.MESH
BF = jnp.bfloat16
F32 = jnp.float32
EPSILON = 1e-6
LOG2E = 1.4426950408889634

NN = (((1,), (0,)), ((), ()))
NT = (((1,), (1,)), ((), ()))
TN = (((0,), (0,)), ((), ()))


def dot(a, b, dims=NN):
    return lax.dot_general(a, b, dims, preferred_element_type=F32)


def mean(v):
    return jnp.mean(v, axis=-1, keepdims=True)


def norm(values):
    centred = values - mean(values)
    inv_std = lax.rsqrt(mean(centred * centred) + EPSILON)
    return centred * inv_std, inv_std


def feature_mean(v):
    return jnp.mean(v, axis=-2, keepdims=True)


def rms_scale(raw):
    return lax.rsqrt(feature_mean(raw * raw) + EPSILON)


def rms_back(grad, raw):
    inv = rms_scale(raw)
    return inv * (grad - raw * (inv * inv) * feature_mean(grad * raw))


def modulate_back(grad, normed, inv_std, table):
    grad_norm = grad * (1.0 + table[1:2, :])
    grad_in = inv_std * (grad_norm - mean(grad_norm) - normed * mean(grad_norm * normed))
    shift = jnp.sum(grad, axis=0, keepdims=True)
    scale = jnp.sum(grad * normed, axis=0, keepdims=True)
    return grad_in, shift, scale


class Sizes:
    pass


def to_blocks(rows, cut):
    n, width = rows.shape[0] // 8, rows.shape[1]
    cube = rows.reshape(n, 8, width)
    low = jnp.concatenate([cube[:, :, cut:], jnp.zeros((n, 8, 2 * cut - width), F32)], axis=2)
    return jnp.concatenate([cube[:, :, :cut], low], axis=1).astype(BF)


def from_blocks(blocks, width):
    n, _, cut = blocks.shape
    cube = blocks.astype(F32)
    full = jnp.concatenate([cube[:, :8, :], cube[:, 8:, : width - cut]], axis=2)
    return full.reshape(n * 8, width)


def to_lines(rows, lines):
    third = rows[0].shape[1] // 3
    parts = [r[:, third * c : third * (c + 1)] for r in rows for c in range(3)]
    if lines > len(parts):
        parts.append(jnp.zeros((lines - len(parts), third), F32))
    return jnp.concatenate(parts, axis=0)


def from_lines(lines, r):
    return jnp.concatenate([lines[3 * r + c : 3 * r + c + 1, :] for c in range(3)], axis=1)


def kernel(z, names, *refs):
    r = Sizes()
    for name, ref in zip(names, refs):
        setattr(r, name, ref)
    heads, hd, width, toks, ns, nt, nz, cut = (
        z.heads, z.hd, z.width, z.toks, z.ns, z.nt, z.nz, z.cut,
    )
    att_w = heads * hd
    hp, pair_w, np_, two = z.hp, 6 * hd, heads // 2, 2 * toks
    scaling = hd ** (-0.5)
    power = scaling * LOG2E
    dp = lax.axis_index("dp")
    tm = lax.axis_index("tm")
    sp = lax.axis_index("space")
    core, y = sp % 2, sp // 2
    x_lo, zz = tm // nz, tm % nz
    x = dp * 2 + x_lo
    nx = 4
    ny = ns // 2

    scope = []

    def phase(name):
        while scope:
            scope.pop().__exit__(None, None, None)
        if name:
            scope.append(jax.named_scope(name))
            scope[-1].__enter__()

    def remote(src, dst, send_sem, recv_sem, device):
        return pltpu.make_async_remote_copy(
            src_ref=src, dst_ref=dst, send_sem=send_sem, recv_sem=recv_sem,
            device_id=device, device_id_type=MESH,
        )

    groups = {
        "space": (ns, sp, lambda j: (dp, tm, j)),
        "tm": (nt, tm, lambda j: (dp, j, sp)),
        "y": (ny, y, lambda j: (dp, tm, j * 2 + core)),
        "x": (nx, x, lambda j: (j // 2, (j % 2) * nz + zz, sp)),
        "z": (nz, zz, lambda j: (dp, x_lo * nz + j, sp)),
    }

    def exchange(group, src_of, recv, sems, d):
        n, me, device = groups[group]
        j = (me + d) % n
        return remote(src_of(j), recv.at[me], sems.at[0, d], sems.at[1, me], device(j))

    def start_all(group, src_of, recv, sems):
        n = groups[group][0]

        def body(d, carry):
            exchange(group, src_of, recv, sems, d).start()
            return carry

        lax.fori_loop(1, n, body, 0)

    def start_to(args, j):
        n, me, _ = groups[args[0]]

        @pl.when(j != me)
        def _():
            exchange(*args, (j - me + n) % n).start()

    def wait_from(group, src_of, recv, sems, j):
        n, me, device = groups[group]
        remote(src_of(j), recv.at[j], sems.at[0, 0], sems.at[1, j], device(j)).wait_recv()

    def wait_other(args, j):
        @pl.when(j != groups[args[0]][1])
        def _():
            wait_from(*args, j)

    def wait_all(group, src_of, recv, sems):
        n, me, _ = groups[group]

        def body(d, carry):
            wait_from(group, src_of, recv, sems, (me + n - d) % n)
            return carry

        lax.fori_loop(1, n, body, 0)

    def wait_sent(group, src_of, recv, sems):
        n = groups[group][0]

        def body(d, carry):
            exchange(group, src_of, recv, sems, d).wait_send()
            return carry

        lax.fori_loop(1, n, body, 0)

    phase("greet")
    pair_order = [(y + d) % np_ for d in range(1, np_ + 1)]

    def rows_of(b):
        return pl.ds(pl.multiple_of(b * pair_w, pair_w), pair_w)

    pair_copies = [
        pltpu.make_async_copy(r.qkv_s.at[rows_of(b)], r.wqs.at[rows_of(b)], r.q_sem.at[i])
        for i, b in enumerate(pair_order)
    ]
    cot_copy, wos_copy, wot_copy, wqt_copy = [
        pltpu.make_async_copy(src, dst, r.w_sem.at[i])
        for i, (src, dst) in enumerate(
            [(r.cot, r.cot_v), (r.out_s, r.wos), (r.out_t, r.wot), (r.qkv_t, r.wqt)]
        )
    ]
    for copy in pair_copies + [cot_copy, wos_copy, wot_copy, wqt_copy]:
        copy.start()
    barrier = pltpu.get_barrier_semaphore()

    def signal(device):
        pl.semaphore_signal(barrier, inc=1, device_id=device, device_id_type=MESH)

    def greet(group):
        n, me, device = groups[group]

        def body(d, carry):
            signal(device((me + d) % n))
            return carry

        lax.fori_loop(1, n, body, 0)

    greet("space")
    greet("tm")
    other = 1 - dp
    signal((other, tm, sp))
    signal((other, (1 - x_lo) * nz + zz, sp))

    phase("norm_space")
    tokens = r.tok[...].astype(F32)
    table_s = r.tab_s[...]
    normed, _ = norm(tokens)
    shifted = (normed * (1.0 + table_s[1:2, :]) + table_s[0:1, :]).astype(BF)
    r.shift_s[...] = shifted

    def gain_columns(ref):
        g = ref[...]
        return [jnp.broadcast_to(g[i : i + 1, :], (toks, hd)).T for i in range(2)]

    gain_s = gain_columns(r.gn_s)
    gain_t = gain_columns(r.gn_t)
    pad_rows = jnp.zeros((hp - hd, toks), F32)
    first_row = lax.broadcasted_iota(jnp.int32, (hp - hd, toks), 0) == 0

    def padded(part):
        return jnp.concatenate([part, pad_rows], axis=0)

    phase("wait_barrier")
    pl.semaphore_wait(barrier, ns - 1 + nt - 1 + 2)
    phase("project_space")
    ps = ("space", lambda j: r.ps_send.at[j], r.ps_recv, r.ps_sem)
    for i, b in enumerate(pair_order):
        pair_copies[i].wait()
        raw = dot(r.wqs[rows_of(b), :], r.shift_s[...], NT)
        r.raw_s[b] = raw
        cube = raw.reshape(6, hd, toks)
        for c in range(2):
            p0, p1, p2 = cube[3 * c], cube[3 * c + 1], cube[3 * c + 2]
            q = p0 * rms_scale(p0) * gain_s[0]
            k = p1 * rms_scale(p1) * gain_s[1]
            r.ps_send[2 * b + c] = jnp.concatenate([q, k, p2, pad_rows], axis=0).astype(BF)
            start_to(ps, 2 * b + c)
    r.ps_recv[sp] = r.ps_send[sp]

    phase("masks")
    own_row = r.val[pl.ds(sp, 1), :].astype(F32)
    row_id = lax.broadcasted_iota(jnp.int32, (toks, toks), 0)
    col_id = lax.broadcasted_iota(jnp.int32, (toks, toks), 1)
    own = jnp.broadcast_to(own_row, (toks, toks))
    mask_s = jnp.sum(jnp.where(row_id == col_id, own, 0.0), axis=1, keepdims=True)
    mask_t = jnp.sum(jnp.where(tm * 8 + row_id % 8 == col_id, own, 0.0), axis=1, keepdims=True)
    cot_copy.wait()
    r.cot_send[...] = to_blocks(r.cot_v[...].astype(F32), cut)
    r.cot_recv[tm] = r.cot_send[tm]
    ct = ("tm", lambda j: r.cot_send.at[j], r.cot_recv, r.cot_sem)

    phase("unpack_packed")

    def unpack(d, carry):
        j = (sp + ns - d) % ns
        wait_other(ps, j)
        block = r.ps_recv[j].astype(F32)
        at = pl.ds(pl.multiple_of(j * toks, toks), toks)
        keys, values = block[hd : 2 * hd, :], block[2 * hd : 3 * hd, :]
        bias = jnp.where(r.val[pl.ds(j, 1), :] > 0, 0.0, -1e30)
        r.q_t[:, at] = jnp.concatenate([block[:hd, :], jnp.where(first_row, 1.0, 0.0)], axis=0).astype(BF)
        r.k_t[:, at] = padded(keys).astype(BF)
        r.v_t[:, at] = padded(values).astype(BF)
        r.k_ref[at, :] = jnp.concatenate([keys, jnp.where(first_row, bias, 0.0)], axis=0).T.astype(BF)
        r.v_ref[at, :] = padded(values).T.astype(BF)
        return carry

    lax.fori_loop(0, ns, unpack, 0)
    start_all(*ct)

    at = ("space", lambda j: r.at_send.at[j], r.at_recv, r.at_sem)

    def two_of(b):
        return pl.ds(pl.multiple_of(b * two, two), two)

    phase("attend_space")
    for b in pair_order:
        scores = dot(r.k_ref[...], r.q_t[:, two_of(b)])
        top = jnp.max(scores, axis=0, keepdims=True)
        exps = jnp.exp2(scores * power - top * power)
        inverse = 1.0 / jnp.sum(exps, axis=0, keepdims=True)
        exps = exps.astype(BF)
        r.prob[b] = exps
        out = dot(r.v_t[...], exps) * inverse
        r.inverse[b] = inverse
        r.o_ref[b] = out
        for c in range(2):
            r.at_send[2 * b + c] = out[:, toks * c : toks * (c + 1)].astype(BF)
            start_to(at, 2 * b + c)
    r.at_recv[sp] = r.at_send[sp]
    phase("wait_attended")
    wait_all(*at)
    phase("out_space")
    att_s = jnp.concatenate([r.at_recv[h].astype(F32)[:hd, :] for h in range(heads)], axis=0).astype(BF)
    r.att_s[...] = att_s
    wos_copy.wait()
    branch_s = dot(att_s, r.wos[...], TN)
    r.branch_s[...] = branch_s
    middle = r.tok[...].astype(F32) + mask_s * table_s[2:3, :] * branch_s
    r.mid_send[...] = to_blocks(middle, cut)
    r.mid_recv[tm] = r.mid_send[tm]
    md = ("tm", lambda j: r.mid_send.at[j], r.mid_recv, r.mid_sem)
    start_all(*md)

    phase("wait_cotangent")
    table_t = r.tab_t[...]
    wait_all(*ct)
    phase("grad_branch_time")
    masked = from_blocks(r.cot_recv[...], width) * mask_t
    grad_branch = (masked * table_t[2:3, :]).astype(BF)
    r.gb_t[...] = grad_branch
    wot_copy.wait()
    r.grad_att[...] = dot(r.wot[...], grad_branch, NT)
    wqt_copy.wait()
    for args in (ps, at, ct):
        wait_sent(*args)

    phase("wait_middle")
    wait_all(*md)
    phase("norm_time")
    normed, _ = norm(from_blocks(r.mid_recv[...], width))
    shifted = (normed * (1.0 + table_t[1:2, :]) + table_t[0:1, :]).astype(BF)
    phase("project_time")
    raw = dot(r.wqt[...], shifted, NT).reshape(heads, 3, hd, toks)
    p0, p1, p2 = raw[:, 0], raw[:, 1], raw[:, 2]
    s0, s1 = rms_scale(p0), rms_scale(p1)
    r.p0[...] = p0
    r.p1[...] = p1
    q = p0 * s0 * gain_t[0][None]
    k = p1 * s1 * gain_t[1][None]
    q_f = [padded(q[h]) for h in range(heads)]
    k_f = [padded(k[h]) for h in range(heads)]
    v_f = [padded(p2[h]) for h in range(heads)]
    q_t, k_t, v_t = ([v.astype(BF) for v in part] for part in (q_f, k_f, v_f))
    phase("attend_time")
    same = (row_id % 8 == col_id % 8)[None]
    scores = jnp.stack([dot(k_f[h].T.astype(BF), q_t[h]) for h in range(heads)], axis=0)
    scores = jnp.where(same, scores, -1e30)
    exps = jnp.exp2((scores - jnp.max(scores, axis=1, keepdims=True)) * power)
    weights = exps * (1.0 / jnp.sum(exps, axis=1, keepdims=True))
    rounded = weights.astype(BF)
    att = jnp.concatenate([dot(v_t[h], rounded[h])[:hd, :] for h in range(heads)], axis=0)
    r.att_t[...] = att.astype(BF)
    phase("attend_back_time")
    do_t = [padded(r.grad_att[hd * h : hd * (h + 1), :]).astype(BF) for h in range(heads)]
    dw = jnp.stack([dot(v_f[h].T.astype(BF), do_t[h]) for h in range(heads)], axis=0)
    ds = weights * (dw - jnp.sum(dw * weights, axis=1, keepdims=True)) * scaling
    ds = ds.astype(BF)

    def stacked(parts):
        return jnp.stack([v[:hd, :] for v in parts], axis=0).astype(BF).astype(F32)

    dq = stacked([dot(k_t[h], ds[h]) for h in range(heads)])
    dk = stacked([dot(q_t[h], ds[h], NT) for h in range(heads)])
    dv = stacked([dot(do_t[h], rounded[h], NT) for h in range(heads)])
    phase("rms_back_time")
    dq = rms_back(dq * gain_t[0][None], r.p0[...])
    dk = rms_back(dk * gain_t[1][None], r.p1[...])
    grad_raw = jnp.stack([dq, dk, dv], axis=1).reshape(3 * att_w, toks).astype(BF)
    phase("back_time")
    grad_shifted = dot(grad_raw, r.wqt[...], TN)
    normed, inv_t = norm(from_blocks(r.mid_recv[...], width))
    grad_in, shift_t, scale_t = modulate_back(grad_shifted, normed, inv_t, table_t)
    r.gm_send[...] = to_blocks(from_blocks(r.cot_recv[...], width) + grad_in, cut)
    r.gm_recv[tm] = r.gm_send[tm]
    gm = ("tm", lambda j: r.gm_send.at[j], r.gm_recv, r.gm_sem)
    start_all(*gm)

    pair = (dp, tm, sp + 1 - 2 * core)

    def pair_copy(a):
        return remote(
            r.part.at[a, 1 - core], r.pair_recv.at[a], r.pair_sem.at[0, a], r.pair_sem.at[1, a], pair
        )

    def partial_grad(a, att, grad_branch):
        full = dot(att, grad_branch)
        pad = jnp.zeros((hp - hd, width), F32)
        for h in range(heads):
            block = jnp.concatenate([full[hd * h : hd * (h + 1), :], pad], axis=0)
            r.part[a, h % 2, h // 2] = block.astype(BF)
        pair_copy(a).start()

    def rs_args(kind, a):
        send, recv, sems = {
            "y": (r.y_send, r.y_recv, r.y_sem),
            "x": (r.x_send, r.x_recv, r.x_sem),
            "z": (r.z_send, r.z_recv, r.z_sem),
        }[kind]
        return (kind, lambda j: send.at[a, j], recv.at[a], sems.at[a])

    def rs_y(a):
        pair_copy(a).wait_recv()
        r.y_send[a] = (r.part[a, core].astype(F32) + r.pair_recv[a].astype(F32)).astype(BF)
        r.y_recv[a, y] = r.y_send[a, y]
        start_all(*rs_args("y", a))

    def total(ref, a, n):
        value = ref[a, 0].astype(F32)
        for j in range(1, n):
            value = value + ref[a, j].astype(F32)
        return value

    def rs_x(a):
        wait_all(*rs_args("y", a))
        value = total(r.y_recv, a, ny)
        part_w = width // nx
        for j in range(nx):
            r.x_send[a, j] = value[:, part_w * j : part_w * (j + 1)].astype(BF)
        r.x_recv[a, x] = r.x_send[a, x]
        start_all(*rs_args("x", a))

    def rs_z(a):
        wait_all(*rs_args("x", a))
        value = total(r.x_recv, a, nx)
        part_w = width // nx // nz
        for j in range(nz):
            r.z_send[a, j] = value[:, part_w * j : part_w * (j + 1)].astype(BF)
        r.z_recv[a, zz] = r.z_send[a, zz]
        start_all(*rs_args("z", a))

    def rs_end(a, out_ref):
        wait_all(*rs_args("z", a))
        out_ref[...] = total(r.z_recv, a, nz)[:hd, :].T

    def table_args(kind, k):
        send, recv, sems = (getattr(r, k + kind + end) for end in ("_send", "_recv", "_sem"))
        return (kind if kind != "s" else "space", lambda j: send, recv, sems)

    def table_start(kind, k, value):
        args = table_args(kind, k)
        getattr(r, k + kind + "_send")[...] = value
        args[2][groups[args[0]][1]] = value
        start_all(*args)

    def table_sum(kind, k):
        args = table_args(kind, k)
        wait_all(*args)
        value = args[2][0]
        for j in range(1, groups[args[0]][0]):
            value = value + args[2][j]
        return value

    phase("partial_time")
    partial_grad(0, r.att_t[...], r.gb_t[...])
    phase("branch_time")
    branch_t = dot(r.att_t[...], r.wot[...], TN)
    middle = from_blocks(r.mid_recv[...], width)
    r.mix_send[...] = to_blocks(middle + mask_t * table_t[2:3, :] * branch_t, cut)
    r.mix_recv[tm] = r.mix_send[tm]
    mx = ("tm", lambda j: r.mix_send.at[j], r.mix_recv, r.mix_sem)
    gate_t = jnp.sum(from_blocks(r.cot_recv[...], width) * mask_t * branch_t, axis=0, keepdims=True)
    phase("pair_time")
    rs_y(0)
    wait_sent(*md)

    phase("wait_grad_middle")
    wait_all(*gm)
    phase("grad_branch_space")
    grad_mid = from_blocks(r.gm_recv[...], width)
    r.grad_mid[...] = grad_mid
    masked = grad_mid * mask_s
    grad_branch = (masked * table_s[2:3, :]).astype(BF)
    r.gb_s[...] = grad_branch
    grad_att = dot(r.wos[...], grad_branch, NT)
    for h in range(heads):
        r.do_send[h] = padded(grad_att[hd * h : hd * (h + 1), :]).astype(BF)
    r.do_recv[sp] = r.do_send[sp]
    do = ("space", lambda j: r.do_send.at[j], r.do_recv, r.do_sem)
    start_all(*do)
    start_all(*mx)
    phase("partial_space")
    partial_grad(1, r.att_s[...], r.gb_s[...])
    gate_s = jnp.sum(r.grad_mid[...] * mask_s * r.branch_s[...], axis=0, keepdims=True)
    table_start("s", "e", to_lines([shift_t, scale_t, gate_t, gate_s], 16))
    phase("rs_x0")
    rs_x(0)

    dqs = ("space", lambda j: r.dq_send.at[j], r.dq_recv, r.dq_sem)
    dks = ("space", lambda j: r.dk_send.at[j], r.dk_recv, r.dk_sem)
    back_order = [(y + np_ - d) % np_ for d in range(np_)]
    for i, b in enumerate(back_order):
        phase("attend_back")
        for c in range(2):
            wait_other(do, 2 * b + c)
        grad_out = jnp.concatenate([r.do_recv[2 * b], r.do_recv[2 * b + 1]], axis=1).astype(F32)
        grad_out = (grad_out * (r.inverse[b] * scaling)).astype(BF)
        shared = jnp.sum(grad_out.astype(F32) * r.o_ref[b], axis=0, keepdims=True)
        exps = r.prob[b]
        ds = (exps.astype(F32) * (dot(r.v_ref[...], grad_out) - shared)).astype(BF)
        dq = dot(r.k_t[...], ds).astype(BF)
        for c in range(2):
            r.dq_send[2 * b + c] = dq[:, toks * c : toks * (c + 1)]
            start_to(dqs, 2 * b + c)
        dv = dot(grad_out, exps, NT)
        dk = dot(r.q_t[:, two_of(b)], ds, NT)
        r.dv_t[...] = dv if i == 0 else r.dv_t[...] + dv
        r.dk_t[...] = dk if i == 0 else r.dk_t[...] + dk
        if i == 1:
            phase("pair_space")
            rs_y(1)
    phase("pack_grads")
    for j in range(ns):
        cols = slice(toks * j, toks * (j + 1))
        r.dk_send[j] = jnp.concatenate(
            [r.dk_t[:hd, cols], r.dv_t[:hd, cols] * (1.0 / scaling)], axis=0
        ).astype(BF)
    start_all(*dks)
    r.dq_recv[sp] = r.dq_send[sp]
    r.dk_recv[sp] = r.dk_send[sp]

    phase("tables_early_x")
    table_start("x", "e", table_sum("s", "e"))
    phase("rs_z0")
    rs_z(0)
    phase("mixed")
    wait_all(*mx)
    r.mixed[...] = from_blocks(r.mix_recv[...], width).astype(BF)
    for args in (gm, do, mx):
        wait_sent(*args)
    pair_copy(0).wait_send()
    for kind in ("y", "x"):
        wait_sent(*rs_args(kind, 0))
    phase("tables_early_z")
    table_start("z", "e", table_sum("x", "e"))

    normed, inv_s = norm(r.tok[...].astype(F32))
    for i, b in enumerate(back_order):
        phase("wait_grad_packed")
        for c in range(2):
            wait_other(dqs, 2 * b + c)
            wait_other(dks, 2 * b + c)
        phase("back_space")
        raw = r.raw_s[b].reshape(6, hd, toks)
        parts = []
        for c in range(2):
            dq = r.dq_recv[2 * b + c].astype(F32)[:hd, :]
            dkv = r.dk_recv[2 * b + c].astype(F32)
            parts.append(rms_back(dq * gain_s[0], raw[3 * c]))
            parts.append(rms_back(dkv[:hd, :] * gain_s[1], raw[3 * c + 1]))
            parts.append(dkv[hd:, :])
        grad_raw = jnp.concatenate(parts, axis=0).astype(BF)
        share = dot(grad_raw, r.wqs[rows_of(b), :], TN)
        r.acc[...] = share if i == 0 else r.acc[...] + share
        if i == 0:
            phase("rs_x1")
            rs_x(1)
    phase("end_space")
    grad_in, shift_s, scale_s = modulate_back(r.acc[...], normed, inv_s, table_s)
    table_start("s", "l", to_lines([shift_s, scale_s], 8))
    r.tgrad[...] = (r.grad_mid[...] + grad_in).astype(BF)
    phase("rs_z1")
    rs_z(1)
    phase("rs_end0")
    rs_end(0, r.got)
    phase("tables_x")
    table_start("x", "l", table_sum("s", "l"))
    early = table_sum("z", "e")
    for args in (dqs, dks):
        wait_sent(*args)
    pair_copy(1).wait_send()
    for args in [rs_args("y", 1), rs_args("x", 1), rs_args("z", 0)]:
        wait_sent(*args)
    for kind in ("s", "x", "z"):
        wait_sent(*table_args(kind, "e"))
    phase("tables_z")
    table_start("z", "l", table_sum("x", "l"))
    phase("rs_end1")
    rs_end(1, r.gos)
    wait_sent(*rs_args("z", 1))
    wait_sent(*table_args("s", "l"))
    wait_sent(*table_args("x", "l"))
    phase("tables_end")
    late = table_sum("z", "l")
    space_rows = [from_lines(late, 0), from_lines(late, 1), from_lines(early, 3)]
    for i in range(3):
        r.tabs[i] = jnp.concatenate([space_rows[i], from_lines(early, i)], axis=0)
    wait_sent(*table_args("z", "l"))
    phase(None)


def hand_on(*refs):
    n = len(refs) // 2
    for i in range(n):
        refs[n + i][...] = refs[i][...]


def solution(mesh):
    nt, ns = mesh.shape["tm"], mesh.shape["space"]

    def on_device(
        tokens, validity, table_space, qkv_space, gains_space, out_space,
        table_time, qkv_time, gains_time, out_time, cotangent,
    ):
        z = Sizes()
        z.width = tokens.shape[3]
        z.toks = tokens.shape[2]
        z.hd = gains_space.shape[1]
        z.heads = out_space.shape[0] // z.hd
        z.ns, z.nt, z.nz = ns, nt, nt // 2
        z.cut = 640
        z.hp = 80
        heads, hd, width, toks, nz, hp = z.heads, z.hd, z.width, z.toks, z.nz, z.hp
        qw, pairs, patches = 3 * heads * hd, ns // 2, ns * toks
        dma = pltpu.SemaphoreType.DMA
        vm = pltpu.VMEM
        third = width // 3
        scratch = {
            "wqs": vm((qw, width), BF),
            "wos": vm((heads * hd, width), BF),
            "wqt": vm((qw, width), BF),
            "wot": vm((heads * hd, width), BF),
            "cot_v": vm((toks, width), BF),
            "q_sem": dma((pairs,)),
            "w_sem": dma((4,)),
            "shift_s": vm((toks, width), BF),
            "raw_s": vm((pairs, 6 * hd, toks), F32),
            "p0": vm((heads, hd, toks), F32),
            "p1": vm((heads, hd, toks), F32),
            "q_t": vm((hp, patches), BF),
            "k_t": vm((hp, patches), BF),
            "v_t": vm((hp, patches), BF),
            "k_ref": vm((patches, hp), BF),
            "v_ref": vm((patches, hp), BF),
            "prob": vm((pairs, patches, 2 * toks), BF),
            "inverse": vm((pairs, 1, 2 * toks), F32),
            "o_ref": vm((pairs, hp, 2 * toks), F32),
            "dk_t": vm((hp, patches), F32),
            "dv_t": vm((hp, patches), F32),
            "att_s": vm((heads * hd, toks), BF),
            "att_t": vm((heads * hd, toks), BF),
            "branch_s": vm((toks, width), F32),
            "grad_att": vm((heads * hd, toks), F32),
            "grad_mid": vm((toks, width), F32),
            "acc": vm((toks, width), F32),
            "gb_t": vm((toks, width), BF),
            "gb_s": vm((toks, width), BF),
            "part": vm((2, 2, pairs, hp, width), BF),
            "pair_recv": vm((2, pairs, hp, width), BF),
            "pair_sem": dma((2, 2)),
        }

        def both(name, n, shape, dtype):
            scratch[name + "_send"] = vm((n,) + shape, dtype)
            scratch[name + "_recv"] = vm((n,) + shape, dtype)
            scratch[name + "_sem"] = dma((2, n))

        both("ps", ns, (3 * hd + 8, toks), BF)
        both("dq", ns, (hp, toks), BF)
        both("dk", ns, (2 * hd, toks), BF)
        both("at", ns, (hp, toks), BF)
        both("do", ns, (hp, toks), BF)
        for name in ("cot", "mid", "gm", "mix"):
            both(name, nt, (16, z.cut), BF)
        for name, n, w in (("y", pairs, width), ("x", 4, width // 4), ("z", nz, width // 4 // nz)):
            scratch[name + "_send"] = vm((2, n, hp, w), BF)
            scratch[name + "_recv"] = vm((2, n, hp, w), BF)
            scratch[name + "_sem"] = dma((2, 2, n))
        for k, lines in (("e", 16), ("l", 8)):
            for kind, n in (("s", ns), ("x", 4), ("z", nz)):
                scratch[k + kind + "_send"] = vm((lines, third), F32)
                scratch[k + kind + "_recv"] = vm((n, lines, third), F32)
                scratch[k + kind + "_sem"] = dma((2, n))

        ins = ["tok", "cot", "val", "tab_s", "gn_s", "tab_t", "gn_t", "qkv_s", "out_s", "qkv_t", "out_t"]
        outs = ["mixed", "tgrad", "gos", "got", "tabs"]
        vmem = pl.BlockSpec(memory_space=pltpu.VMEM)
        anywhere = pl.BlockSpec(memory_space=pl.ANY)
        results = pl.pallas_call(
            functools.partial(kernel, z, ins + outs + list(scratch)),
            out_shape=[
                jax.ShapeDtypeStruct((toks, width), BF),
                jax.ShapeDtypeStruct((toks, width), BF),
                jax.ShapeDtypeStruct((width // 4 // nz, hd), F32),
                jax.ShapeDtypeStruct((width // 4 // nz, hd), F32),
                jax.ShapeDtypeStruct((3, 2, width), F32),
            ],
            in_specs=[vmem] + [anywhere] + [vmem] * 5 + [anywhere] * 4,
            out_specs=[vmem] * 5,
            scratch_shapes=list(scratch.values()),
            compiler_params=pltpu.CompilerParams(
                collective_id=0, has_side_effects=True, vmem_limit_bytes=56 * 1024 * 1024
            ),
        )(
            tokens.reshape(toks, width),
            cotangent.reshape(toks, width),
            validity.reshape(ns, toks),
            table_space,
            gains_space,
            table_time,
            gains_time,
            qkv_space.T,
            out_space,
            qkv_time.T,
            out_time,
        )
        mixed, tgrad, gos, got, tabs = pl.pallas_call(
            hand_on,
            out_shape=[jax.ShapeDtypeStruct(v.shape, v.dtype) for v in results],
            in_specs=[vmem] * 5,
            out_specs=[vmem] * 5,
        )(*results)
        shape = tokens.shape
        return mixed.reshape(shape), tgrad.reshape(shape), gos.T, got.T, tabs.transpose(1, 0, 2)

    spread = P("dp", "tm", "space", None)
    return jax.shard_map(
        on_device,
        mesh=mesh,
        in_specs=(spread,) + (P(),) * 9 + (spread,),
        out_specs=(spread, spread, P("space", ("dp", "tm")), P("space", ("dp", "tm")), P()),
        check_vma=False,
    )
```

```python
import functools

import jax
import jax.numpy as jnp
from jax import lax
from jax.experimental import pallas as pl
from jax.experimental.pallas import tpu as pltpu
from jax.sharding import PartitionSpec as P

MESH = pl.DeviceIdType.MESH
BF = jnp.bfloat16
F32 = jnp.float32
EPSILON = 1e-6
LOG2E = 1.4426950408889634

NN = (((1,), (0,)), ((), ()))
NT = (((1,), (1,)), ((), ()))
TN = (((0,), (0,)), ((), ()))


def dot(a, b, dims=NN):
    return lax.dot_general(a, b, dims, preferred_element_type=F32)


def mean(v):
    return jnp.mean(v, axis=-1, keepdims=True)


def norm(values):
    centred = values - mean(values)
    inv_std = lax.rsqrt(mean(centred * centred) + EPSILON)
    return centred * inv_std, inv_std


def feature_mean(v):
    return jnp.mean(v, axis=-2, keepdims=True)


def rms_scale(raw):
    return lax.rsqrt(feature_mean(raw * raw) + EPSILON)


def rms_back(grad, raw):
    inv = rms_scale(raw)
    return inv * (grad - raw * (inv * inv) * feature_mean(grad * raw))


def modulate_back(grad, normed, inv_std, table):
    grad_norm = grad * (1.0 + table[1:2, :])
    grad_in = inv_std * (grad_norm - mean(grad_norm) - normed * mean(grad_norm * normed))
    shift = jnp.sum(grad, axis=0, keepdims=True)
    scale = jnp.sum(grad * normed, axis=0, keepdims=True)
    return grad_in, shift, scale


class Sizes:
    pass


def to_blocks(rows):
    n, width = rows.shape[0] // 8, rows.shape[1]
    cube = rows.reshape(n, 8, width)
    return jnp.concatenate([cube[:, :, c : c + 128] for c in range(0, width, 128)], axis=1).astype(BF)


def from_blocks(blocks):
    n, lines, _ = blocks.shape
    cube = blocks.astype(F32)
    full = jnp.concatenate([cube[:, c : c + 8, :] for c in range(0, lines, 8)], axis=2)
    return full.reshape(n * 8, lines * 16)


def to_lines(rows, lines):
    parts = [r[:, c : c + 128] for r in rows for c in range(0, rows[0].shape[1], 128)]
    if lines > len(parts):
        parts.append(jnp.zeros((lines - len(parts), 128), F32))
    return jnp.concatenate(parts, axis=0)


def from_lines(lines, r, n):
    return jnp.concatenate([lines[n * r + c : n * r + c + 1, :] for c in range(n)], axis=1)


def kernel(z, names, *refs):
    r = Sizes()
    for name, ref in zip(names, refs):
        setattr(r, name, ref)
    heads, hd, width, toks, ns, nt, nz = (
        z.heads, z.hd, z.width, z.toks, z.ns, z.nt, z.nz,
    )
    att_w = heads * hd
    hp, pair_w, np_, two = z.hp, 6 * hd, heads // 2, 2 * toks
    scaling = hd ** (-0.5)
    power = scaling * LOG2E
    dp = lax.axis_index("dp")
    tm = lax.axis_index("tm")
    sp = lax.axis_index("space")
    core, y = sp % 2, sp // 2
    sibling = sp + 1 - 2 * core
    x_lo, zz = tm // nz, tm % nz
    x = dp * 2 + x_lo
    nx = 4
    ny = ns // 2

    def remote(src, dst, send_sem, recv_sem, device):
        return pltpu.make_async_remote_copy(
            src_ref=src, dst_ref=dst, send_sem=send_sem, recv_sem=recv_sem,
            device_id=device, device_id_type=MESH,
        )

    groups = {
        "space": (ns, sp, lambda j: (dp, tm, j)),
        "tm": (nt, tm, lambda j: (dp, j, sp)),
        "y": (ny, y, lambda j: (dp, tm, j * 2 + core)),
        "x": (nx, x, lambda j: (j // 2, (j % 2) * nz + zz, sp)),
        "z": (nz, zz, lambda j: (dp, x_lo * nz + j, sp)),
    }

    def exchange(group, src_of, recv, sems, d, each=False):
        n, me, device = groups[group]
        j = (me + d) % n
        arrived = sems.at[1 + me] if each else sems.at[1]
        return remote(src_of(j), recv.at[me], sems.at[0], arrived, device(j))

    def whole(group, src_of, recv, sems, each=False):
        n, me, device = groups[group]
        part = recv.at[pl.ds(0, n - 1)]
        return remote(part, part, sems.at[0], sems.at[1], device((me + 1) % n))

    ring = [4, 3, 5, 2, 6, 1, 7]
    order = {
        "space": ring,
        "z": ring,
        "x": [2, 1, 3],
        "y": [2, 1, 3],
        "tm": [d + h for d in ring for h in (0, nz)] + [nz],
    }

    def start_all(group, src_of, recv, sems, each=False):
        for d in order[group]:
            exchange(group, src_of, recv, sems, d, each).start()

    def start_to(args, j):
        n, me, _ = groups[args[0]]
        exchange(*args[:4], (j - me + n) % n, *args[4:]).start()

    def wait_from(group, src_of, recv, sems, each, j):
        device = groups[group][2]
        remote(src_of(j), recv.at[j], sems.at[0], sems.at[1 + j], device(j)).wait_recv()

    def wait_all(*args):
        whole(*args).wait_recv()

    def wait_sent(*args):
        whole(*args).wait_send()

    barrier = pltpu.get_barrier_semaphore()

    def signal(device):
        pl.semaphore_signal(barrier, inc=1, device_id=device, device_id_type=MESH)

    def greet(group):
        n, me, device = groups[group]

        def body(d, carry):
            signal(device((me + d) % n))
            return carry

        lax.fori_loop(1, n, body, 0)

    pair_order = [(y + d) % np_ for d in (2, 1, 3, 0)]

    def rows_of(b):
        return pl.ds(pl.multiple_of(b * pair_w, pair_w), pair_w)

    results = [
        pltpu.make_async_copy(src, dst, r.o_sem.at[i])
        for i, (src, dst) in enumerate(
            [
                (r.mixed, r.mixed_out),
                (r.tgrad, r.tgrad_out),
                (r.gos, r.gos_out),
                (r.got, r.got_out),
                (r.tabs, r.tabs_out),
            ]
        )
    ]
    pair_copies = [
        pltpu.make_async_copy(r.qkv_s.at[rows_of(b)], r.wqs.at[rows_of(b)], r.q_sem.at[i])
        for i, b in enumerate(pair_order)
    ]
    copies = {
        name: pltpu.make_async_copy(src, dst, r.w_sem.at[i])
        for i, (name, src, dst) in enumerate(
            [
                ("tok", r.tok_in, r.tok),
                ("tab_s", r.tab_s_in, r.tab_s),
                ("gn_s", r.gn_s_in, r.gn_s),
                ("val", r.val_in, r.val),
                ("cot", r.cot_in, r.cot),
                ("tab_t", r.tab_t_in, r.tab_t),
                ("gn_t", r.gn_t_in, r.gn_t),
                ("wos", r.out_s, r.wos),
                ("wot", r.out_t, r.wot),
                ("wqt", r.qkv_t, r.wqt),
            ]
        )
    }
    for name in ("tok", "tab_s", "gn_s"):
        copies[name].start()
    pair_copies[0].start()
    greet("space")
    greet("tm")
    other = 1 - dp
    signal((other, tm, sp))
    signal((other, (1 - x_lo) * nz + zz, sp))
    for copy in pair_copies[1:]:
        copy.start()
    for name in ("val", "cot", "tab_t", "gn_t", "wos", "wot", "wqt"):
        copies[name].start()

    copies["tok"].wait()
    copies["tab_s"].wait()
    tokens = r.tok[...].astype(F32)
    table_s = r.tab_s[...]
    normed, _ = norm(tokens)
    shifted = (normed * (1.0 + table_s[1:2, :]) + table_s[0:1, :]).astype(BF)
    r.shift_s[...] = shifted

    def gain_columns(ref):
        g = ref[...]
        return [jnp.broadcast_to(g[i : i + 1, :], (toks, hd)).T for i in range(2)]

    copies["gn_s"].wait()
    gain_s = gain_columns(r.gn_s)
    pad_rows = jnp.zeros((hp - hd, toks), F32)
    first_row = lax.broadcasted_iota(jnp.int32, (hp - hd, toks), 0) == 0

    def padded(part):
        return jnp.concatenate([part, pad_rows], axis=0)

    kv = ("space", lambda j: r.kv_send.at[j], r.kv_recv, r.kv_sem, True)
    qs = ("space", lambda j: r.qs_send.at[j], r.qs_recv, r.qs_sem, True)

    def project_pair(i, b):
        pair_copies[i].wait()
        raw = dot(r.shift_s[...], r.wqs[rows_of(b), :], NT).T
        r.raw_s[b] = raw
        cube = raw.reshape(6, hd, toks)
        for c in range(2):
            p0, p1, p2 = cube[3 * c], cube[3 * c + 1], cube[3 * c + 2]
            q = p0 * rms_scale(p0) * gain_s[0]
            k = p1 * rms_scale(p1) * gain_s[1]
            r.qs_send[2 * b + c] = q.astype(BF)
            r.kv_send[2 * b + c] = jnp.concatenate([k, p2], axis=0).astype(BF)

    def start_pair(args, i, b):
        if i < np_ - 1:
            start_to(args, 2 * b)
            start_to(args, 2 * b + 1)
        else:
            start_to(args, sibling)

    project_pair(0, pair_order[0])
    r.tk_send[...] = to_blocks(r.tok[...].astype(F32))
    r.tk_recv[tm] = r.tk_send[tm]
    tk = ("tm", lambda j: r.tk_send.at[j], r.tk_recv, r.tk_sem)
    pl.semaphore_wait(barrier, ns - 1 + nt - 1 + 2)
    start_pair(kv, 0, pair_order[0])
    start_all(*tk)
    for i in range(1, np_):
        project_pair(i, pair_order[i])
        start_pair(kv, i, pair_order[i])
    for i in range(np_):
        start_pair(qs, i, pair_order[i])
    r.kv_recv[sp] = r.kv_send[sp]
    r.qs_recv[sp] = r.qs_send[sp]

    copies["cot"].wait()
    r.cot_send[...] = to_blocks(r.cot[...].astype(F32))
    r.cot_recv[tm] = r.cot_send[tm]
    ct = ("tm", lambda j: r.cot_send.at[j], r.cot_recv, r.cot_sem)
    start_all(*ct)
    copies["val"].wait()
    own_row = r.val[pl.ds(sp, 1), :].astype(F32)
    row_id = lax.broadcasted_iota(jnp.int32, (toks, toks), 0)
    col_id = lax.broadcasted_iota(jnp.int32, (toks, toks), 1)
    own = jnp.broadcast_to(own_row, (toks, toks))
    mask_s = jnp.sum(jnp.where(row_id == col_id, own, 0.0), axis=1, keepdims=True)
    mask_t = jnp.sum(jnp.where(tm * 8 + row_id % 8 == col_id, own, 0.0), axis=1, keepdims=True)


    def unpack(j):
        block = r.kv_recv[j].astype(F32)
        at = pl.ds(pl.multiple_of(j * toks, toks), toks)
        keys, values = block[:hd, :], block[hd:, :]
        bias = jnp.where(r.val[pl.ds(j, 1), :] > 0, 0.0, -1e30)
        r.k_t[:, at] = padded(keys).astype(BF)
        r.v_t[:, at] = padded(values).astype(BF)
        r.k_ref[at, :] = jnp.concatenate([keys, jnp.where(first_row, bias, 0.0)], axis=0).T.astype(BF)
        r.v_ref[at, :] = padded(values).T.astype(BF)

    unpack(sp)
    for b in pair_order[::-1]:
        for j in [sibling] if b is pair_order[-1] else [2 * b, 2 * b + 1]:
            wait_from(*kv, j)
            unpack(j)

    at = ("space", lambda j: r.at_send.at[j], r.at_recv, r.at_sem)

    def two_of(b):
        return pl.ds(pl.multiple_of(b * two, two), two)

    ones = jnp.where(lax.broadcasted_iota(jnp.int32, (hp - hd, two), 0) == 0, 1.0, 0.0)

    def scores_of(i, b):
        for j in [sibling] if i == 0 else [2 * b, 2 * b + 1]:
            wait_from(*qs, j)
        q = jnp.concatenate([r.qs_recv[2 * b + c].astype(F32) for c in range(2)], axis=1)
        r.q_t[:, two_of(b)] = jnp.concatenate([q, ones], axis=0).astype(BF)
        return dot(r.k_ref[...], r.q_t[:, two_of(b)])

    attend_order = [(y + d) % np_ for d in (0, 2, 1, 3)]
    following = scores_of(0, attend_order[0])
    for i, b in enumerate(attend_order):
        scores = following
        top = jnp.max(scores, axis=0, keepdims=True)
        if i < np_ - 1:
            following = scores_of(i + 1, attend_order[i + 1])
        exps = jnp.exp2(scores * power - top * power)
        inverse = 1.0 / jnp.sum(exps, axis=0, keepdims=True)
        exps = exps.astype(BF)
        r.prob[b] = exps
        out = dot(r.v_t[...], exps) * inverse
        r.inverse[b] = inverse
        r.o_ref[b] = out
        for c in range(2):
            r.at_send[2 * b + c] = out[:hd, toks * c : toks * (c + 1)].astype(BF)
        start_pair(at, np_ - 1 if i == 0 else 0, b)
    r.at_recv[sp] = r.at_send[sp]
    wait_all(*at)
    fill = jnp.zeros((z.att_pad - att_w, toks), F32)

    att = jnp.concatenate([r.at_recv[h].astype(F32) for h in range(heads)] + [fill], axis=0).T
    r.aa_send[...] = to_blocks(att)
    r.aa_recv[tm] = r.aa_send[tm]
    aa = ("tm", lambda j: r.aa_send.at[j], r.aa_recv, r.aa_sem)
    start_all(*aa)
    copies["wos"].wait()
    branch = dot(att[:, :att_w].astype(BF), r.wos[...])
    r.mid_o[...] = (r.tok[...].astype(F32) + mask_s * table_s[2:3, :] * branch).astype(BF)

    pair = (dp, tm, sibling)

    def pair_copy(a):
        return remote(
            r.part.at[a, 1 - core], r.pair_recv.at[a], r.pair_sem.at[0, a], r.pair_sem.at[1, a], pair
        )

    def partial_grad(a, att, grad_branch, dims=NN):
        full = dot(att, grad_branch, dims)
        for h in range(heads):
            r.part[a, h % 2, h // 2] = full[hd * h : hd * (h + 1), :].astype(BF)
        pair_copy(a).start()

    def rs_args(kind, a):
        send, recv, sems = (getattr(r, kind + str(a) + end) for end in ("_send", "_recv", "_sem"))
        return (kind, lambda j: send.at[j], recv, sems)

    def total(ref, n):
        value = ref[0].astype(F32)
        for j in range(1, n):
            value = value + ref[j].astype(F32)
        return value

    quarter = width // nx
    rest = quarter - 256

    def rs_y0():
        pair_copy(0).wait_recv()
        for b in range(ny):
            r.y0_send[b] = (r.part[0, core, b].astype(F32) + r.pair_recv[0, b].astype(F32)).astype(BF)
        r.y0_recv[y] = r.y0_send[y]
        start_all(*rs_args("y", 0))

    def rs_x0():
        wait_all(*rs_args("y", 0))
        value = total(r.y0_recv, ny)
        for j in range(nx):
            r.x0_send[j] = value[:, quarter * j : quarter * (j + 1)].astype(BF)
        r.x0_recv[x] = r.x0_send[x]
        start_all(*rs_args("x", 0))

    def rs_x1():
        pair_copy(1).wait_recv()
        value = [r.part[1, core, b].astype(F32) + r.pair_recv[1, b].astype(F32) for b in range(ny)]
        for j in range(nx):
            cols = [v[:, quarter * j : quarter * (j + 1)] for v in value]
            for b in range(ny):
                r.x1_send[j, 2 * b] = cols[b][:, :128].astype(BF)
                r.x1_send[j, 2 * b + 1] = cols[b][:, 128:256].astype(BF)
            r.x1_send[j, 2 * ny] = jnp.concatenate([v[:, 256:] for v in cols], axis=1).astype(BF)
        r.x1_recv[x] = r.x1_send[x]
        start_all(*rs_args("x", 1))

    def rs_y1():
        wait_all(*rs_args("x", 1))
        value = total(r.x1_recv, nx)
        for b in range(ny):
            tail = value[2 * ny][:, rest * b : rest * (b + 1)]
            r.y1_send[b] = jnp.concatenate([value[2 * b], value[2 * b + 1], tail], axis=1).astype(BF)
        r.y1_recv[y] = r.y1_send[y]
        start_all(*rs_args("y", 1))

    third = hd // 3
    own_w = quarter // nz

    def rs_z(a):
        wait_all(*rs_args("x" if a == 0 else "y", a))
        value = total(r.x0_recv, nx) if a == 0 else total(r.y1_recv, ny)
        _, send_of, recv, _ = rs_args("z", a)
        fill = jnp.zeros((third, 128 - 3 * own_w), F32)
        for j in range(nz):
            cols = value[:, own_w * j : own_w * (j + 1)]
            parts = [cols[third * c : third * (c + 1), :] for c in range(3)]
            send_of(j)[...] = jnp.concatenate(parts + [fill], axis=1).astype(BF)
        recv[zz] = send_of(zz)[...]
        start_all(*rs_args("z", a))

    def rs_end(a, out_ref):
        wait_all(*rs_args("z", a))
        value = total(rs_args("z", a)[2], nz)
        cols = [value[:, own_w * c : own_w * (c + 1)] for c in range(3)]
        out_ref[...] = jnp.concatenate(cols, axis=0).T

    def table_args(kind, k):
        send, recv, sems = (getattr(r, k + kind + end) for end in ("_send", "_recv", "_sem"))
        return ({"s": "space", "a": "x"}.get(kind, kind), lambda j: send, recv, sems)

    def table_start(kind, k, value):
        args = table_args(kind, k)
        send = getattr(r, k + kind + "_send")
        send[...] = value.astype(send.dtype)
        args[2][groups[args[0]][1]] = send[...]
        start_all(*args)

    def table_sum(kind, k):
        args = table_args(kind, k)
        wait_all(*args)
        value = args[2][0].astype(F32)
        for j in range(1, groups[args[0]][0]):
            value = value + args[2][j].astype(F32)
        return value

    copies["tab_t"].wait()
    table_t = r.tab_t[...]
    wait_all(*tk)
    wait_all(*ct)
    masked = from_blocks(r.cot_recv[...]) * mask_t
    grad_branch = (masked * table_t[2:3, :]).astype(BF)
    r.gb_t[...] = grad_branch
    copies["wot"].wait()
    r.grad_att[...] = dot(r.wot[...], grad_branch, NT)
    copies["wqt"].wait()
    copies["gn_t"].wait()
    gain_t = gain_columns(r.gn_t)
    for args in (kv, qs, at, tk, ct):
        wait_sent(*args)

    wait_all(*aa)
    att_s = from_blocks(r.aa_recv[...])[:, :att_w].astype(BF)
    r.att_s[...] = att_s
    branch_s = dot(att_s, r.wos[...])
    r.branch_s[...] = branch_s
    middle = from_blocks(r.tk_recv[...]) + mask_t * table_s[2:3, :] * branch_s
    r.mid[...] = middle.astype(BF)
    normed, _ = norm(r.mid[...].astype(F32))
    shifted = (normed * (1.0 + table_t[1:2, :]) + table_t[0:1, :]).astype(BF)
    raw = dot(shifted, r.wqt[...], NT).T.reshape(heads, 3, hd, toks)
    p0, p1, p2 = raw[:, 0], raw[:, 1], raw[:, 2]
    s0, s1 = rms_scale(p0), rms_scale(p1)
    r.p0[...] = p0
    r.p1[...] = p1
    q = p0 * s0 * gain_t[0][None]
    k = p1 * s1 * gain_t[1][None]
    q_f = [padded(q[h]) for h in range(heads)]
    k_f = [padded(k[h]) for h in range(heads)]
    v_f = [padded(p2[h]) for h in range(heads)]
    q_t, k_t, v_t = ([v.astype(BF) for v in part] for part in (q_f, k_f, v_f))
    same = (row_id % 8 == col_id % 8)[None]
    scores = jnp.stack([dot(k_f[h].T.astype(BF), q_t[h]) for h in range(heads)], axis=0)
    scores = jnp.where(same, scores, -1e30)
    exps = jnp.exp2((scores - jnp.max(scores, axis=1, keepdims=True)) * power)
    weights = exps * (1.0 / jnp.sum(exps, axis=1, keepdims=True))
    rounded = weights.astype(BF)
    att = jnp.concatenate([dot(v_t[h], rounded[h])[:hd, :] for h in range(heads)] + [fill], axis=0)
    r.att_f[...] = att
    r.att_t[...] = att[:att_w, :].astype(BF)
    partial_grad(0, r.att_t[...], r.gb_t[...])
    do_t = [padded(r.grad_att[hd * h : hd * (h + 1), :]).astype(BF) for h in range(heads)]
    dw = jnp.stack([dot(v_f[h].T.astype(BF), do_t[h]) for h in range(heads)], axis=0)
    ds = weights * (dw - jnp.sum(dw * weights, axis=1, keepdims=True)) * scaling
    ds = ds.astype(BF)

    def stacked(parts):
        return jnp.stack([v[:hd, :] for v in parts], axis=0).astype(BF).astype(F32)

    dq = stacked([dot(k_t[h], ds[h]) for h in range(heads)])
    dk = stacked([dot(q_t[h], ds[h], NT) for h in range(heads)])
    dv = stacked([dot(do_t[h], rounded[h], NT) for h in range(heads)])
    dq = rms_back(dq * gain_t[0][None], r.p0[...])
    dk = rms_back(dk * gain_t[1][None], r.p1[...])
    grad_raw = jnp.stack([dq, dk, dv], axis=1).reshape(3 * att_w, toks).astype(BF)
    grad_shifted = dot(grad_raw, r.wqt[...], TN)
    normed, inv_t = norm(r.mid[...].astype(F32))
    grad_in, shift_t, scale_t = modulate_back(grad_shifted, normed, inv_t, table_t)
    grad_mid = (from_blocks(r.cot_recv[...]) + grad_in).astype(BF).astype(F32)
    r.grad_mid[...] = grad_mid
    rs_y0()
    grad_branch = (grad_mid * mask_t * table_s[2:3, :]).astype(BF)
    r.gb_s[...] = grad_branch
    grad_att = dot(grad_branch, r.wos[...], NT)
    r.ga_send[...] = to_blocks(
        jnp.concatenate([grad_att, jnp.zeros((toks, z.att_pad - att_w), F32)], axis=1)
    )
    r.ga_recv[tm] = r.ga_send[tm]
    ga = ("tm", lambda j: r.ga_send.at[j], r.ga_recv, r.ga_sem)
    start_all(*ga)

    partial_grad(1, r.att_s[...], r.gb_s[...], TN)
    branch_t = dot(r.att_t[...], r.wot[...], TN)
    gate_t = jnp.sum(from_blocks(r.cot_recv[...]) * mask_t * branch_t, axis=0, keepdims=True)
    gate_s = jnp.sum(r.grad_mid[...] * mask_t * r.branch_s[...], axis=0, keepdims=True)
    r.gm_send[...] = to_blocks(r.grad_mid[...])
    r.gm_recv[tm] = r.gm_send[tm]
    gm = ("tm", lambda j: r.gm_send.at[j], r.gm_recv, r.gm_sem)
    r.ta_send[...] = to_blocks(r.att_f[...].T)
    r.ta_recv[tm] = r.ta_send[tm]
    ta = ("tm", lambda j: r.ta_send.at[j], r.ta_recv, r.ta_sem)
    rs_x1()
    wait_sent(*aa)

    wait_all(*ga)
    grad_att = from_blocks(r.ga_recv[...]).T
    for h in range(heads):
        r.do_send[h] = grad_att[hd * h : hd * (h + 1), :].astype(BF)
    r.do_recv[sp] = r.do_send[sp]
    do = ("space", lambda j: r.do_send.at[j], r.do_recv, r.do_sem, True)
    start_all(*do)
    table_start("s", "e", to_lines([shift_t, scale_t, gate_t, gate_s], z.early))

    lines = width // 128
    ex = ("x", lambda j: r.ex_send.at[j], r.ex_recv, r.ex_sem)

    def early_x():
        value = table_sum("s", "e")
        blank = jnp.zeros((16 - lines, 128), F32)
        for j in range(nx):
            r.ex_send[j] = jnp.concatenate([value[lines * j : lines * (j + 1), :], blank], axis=0)
        r.ex_recv[x] = r.ex_send[x]
        start_all(*ex)

    def early_z():
        wait_all(*ex)
        table_start("z", "e", r.ex_recv[0] + r.ex_recv[1] + r.ex_recv[2] + r.ex_recv[3])

    dqs = ("space", lambda j: r.dq_send.at[j], r.dq_recv, r.dq_sem, True)
    dks = ("space", lambda j: r.dk_send.at[j], r.dk_recv, r.dk_sem, True)
    back_order = [(y + d) % np_ for d in (0, 1, 3, 2)]
    for i, b in enumerate(back_order):
        for j in [sibling] if i == 0 else [2 * b, 2 * b + 1]:
            wait_from(*do, j)
        grad_out = jnp.concatenate([r.do_recv[2 * b + c].astype(F32) for c in range(2)], axis=1)
        grad_out = grad_out * (r.inverse[b] * scaling)
        grad_out = jnp.concatenate([grad_out, jnp.zeros((hp - hd, two), F32)], axis=0).astype(BF)
        shared = jnp.sum(grad_out.astype(F32) * r.o_ref[b], axis=0, keepdims=True)
        exps = r.prob[b]
        ds = (exps.astype(F32) * (dot(r.v_ref[...], grad_out) - shared)).astype(BF)
        dq = dot(r.k_t[...], ds)
        for c in range(2):
            r.dq_send[2 * b + c] = dq[:hd, toks * c : toks * (c + 1)].astype(BF)
        start_pair(dqs, np_ - 1 if i == 0 else 0, b)
        dv = dot(grad_out, exps, NT)
        dk = dot(r.q_t[:, two_of(b)], ds, NT)
        r.dv_t[...] = dv if i == 0 else r.dv_t[...] + dv
        r.dk_t[...] = dk if i == 0 else r.dk_t[...] + dk
        if i == 0:
            start_all(*gm)
        if i == 2:
            rs_x0()
            start_all(*ta)
    for j in range(ns):
        cols = slice(toks * j, toks * (j + 1))
        r.dk_send[j] = jnp.concatenate(
            [r.dk_t[:hd, cols], r.dv_t[:hd, cols] * (1.0 / scaling)], axis=0
        ).astype(BF)
    start_all(*dks)
    r.dq_recv[sp] = r.dq_send[sp]
    r.dk_recv[sp] = r.dk_send[sp]

    rs_y1()
    early_x()
    for args in (ga, do):
        wait_sent(*args)
    pair_copy(0).wait_send()
    pair_copy(1).wait_send()

    normed, inv_s = norm(r.tok[...].astype(F32))
    for i, b in enumerate(back_order):
        for j in [sibling] if i == 0 else [2 * b, 2 * b + 1]:
            wait_from(*dqs, j)
            wait_from(*dks, j)
        raw = r.raw_s[b].reshape(6, hd, toks)
        parts = []
        for c in range(2):
            dq = r.dq_recv[2 * b + c].astype(F32)
            dkv = r.dk_recv[2 * b + c].astype(F32)
            parts.append(rms_back(dq * gain_s[0], raw[3 * c]))
            parts.append(rms_back(dkv[:hd, :] * gain_s[1], raw[3 * c + 1]))
            parts.append(dkv[hd:, :])
        grad_raw = jnp.concatenate(parts, axis=0).astype(BF)
        share = dot(grad_raw, r.wqs[rows_of(b), :], TN)
        r.acc[...] = share if i == 0 else r.acc[...] + share
    grad_in, shift_s, scale_s = modulate_back(r.acc[...], normed, inv_s, table_s)
    table_start("s", "l", to_lines([shift_s, scale_s], z.late))
    rs_z(0)
    table_start("x", "l", table_sum("s", "l"))
    early_z()
    rs_z(1)
    wait_all(*gm)
    r.tgrad[...] = (from_blocks(r.gm_recv[...]) + grad_in).astype(BF)
    results[1].start()
    table_start("z", "l", table_sum("x", "l"))
    wait_all(*ta)
    branch = dot(from_blocks(r.ta_recv[...])[:, :att_w].astype(BF), r.wot[...])
    mixed = r.mid_o[...].astype(F32) + mask_s * table_t[2:3, :] * branch
    r.mixed[...] = mixed.astype(BF)
    results[0].start()
    for args in (dqs, dks, gm, ta, ex):
        wait_sent(*args)
    for a in range(2):
        wait_sent(*rs_args("x", a))
    for a in range(2):
        wait_sent(*rs_args("y", a))
    for args in [table_args("s", "e"), table_args("z", "e"), table_args("s", "l"), table_args("x", "l")]:
        wait_sent(*args)
    wait_sent(*rs_args("z", 0))
    table_start("a", "e", table_sum("z", "e"))
    rs_end(0, r.got)
    results[3].start()
    wait_all(*table_args("a", "e"))
    rs_end(1, r.gos)
    results[2].start()
    wait_sent(*rs_args("z", 1))
    wait_sent(*table_args("a", "e"))
    late = table_sum("z", "l")
    space_rows = [from_lines(late, 0, lines), from_lines(late, 1, lines), from_lines(r.ea_recv[3], 0, lines)]
    for i in range(3):
        r.tabs[i] = jnp.concatenate([space_rows[i], from_lines(r.ea_recv[i], 0, lines)], axis=0)
    results[4].start()
    wait_sent(*table_args("z", "l"))
    for copy in results:
        copy.wait()


def hand_on(*refs):
    n = (len(refs) - 2) // 3
    srcs, dsts, stages, (into, out) = refs[:n], refs[n : 2 * n], refs[2 * n : 3 * n], refs[3 * n :]
    first = [pltpu.make_async_copy(srcs[i], stages[i], into.at[i]) for i in range(n)]
    second = [pltpu.make_async_copy(stages[i], dsts[i], out.at[i]) for i in range(n)]
    for copy in first:
        copy.start()
    for i in range(n):
        first[i].wait()
        second[i].start()
    for copy in second:
        copy.wait()


def solution(mesh):
    nt, ns = mesh.shape["tm"], mesh.shape["space"]

    def on_device(
        tokens, validity, table_space, qkv_space, gains_space, out_space,
        table_time, qkv_time, gains_time, out_time, cotangent,
    ):
        z = Sizes()
        z.width = tokens.shape[3]
        z.toks = tokens.shape[2]
        z.hd = gains_space.shape[1]
        z.heads = out_space.shape[0] // z.hd
        z.ns, z.nt, z.nz = ns, nt, nt // 2
        z.hp = 80
        heads, hd, width, toks, nz, hp = z.heads, z.hd, z.width, z.toks, z.nz, z.hp
        qw, pairs, patches = 3 * heads * hd, ns // 2, ns * toks
        dma = pltpu.SemaphoreType.DMA
        vm = pltpu.VMEM
        z.att_pad = -(-heads * hd // 128) * 128
        z.early, z.late = 40, 32
        scratch = {
            "wqs": vm((qw, width), BF),
            "wos": vm((heads * hd, width), BF),
            "wqt": vm((qw, width), BF),
            "wot": vm((heads * hd, width), BF),
            "tok": vm((toks, width), BF),
            "cot": vm((toks, width), BF),
            "val": vm((ns, toks), jnp.int32),
            "tab_s": vm((3, width), F32),
            "tab_t": vm((3, width), F32),
            "gn_s": vm((2, hd), F32),
            "gn_t": vm((2, hd), F32),
            "q_sem": dma((pairs,)),
            "w_sem": dma((10,)),
            "shift_s": vm((toks, width), BF),
            "raw_s": vm((pairs, 6 * hd, toks), F32),
            "p0": vm((heads, hd, toks), F32),
            "p1": vm((heads, hd, toks), F32),
            "q_t": vm((hp, patches), BF),
            "k_t": vm((hp, patches), BF),
            "v_t": vm((hp, patches), BF),
            "k_ref": vm((patches, hp), BF),
            "v_ref": vm((patches, hp), BF),
            "prob": vm((pairs, patches, 2 * toks), BF),
            "inverse": vm((pairs, 1, 2 * toks), F32),
            "o_ref": vm((pairs, hp, 2 * toks), F32),
            "dk_t": vm((hp, patches), F32),
            "dv_t": vm((hp, patches), F32),
            "att_s": vm((toks, heads * hd), BF),
            "mid": vm((toks, width), BF),
            "mid_o": vm((toks, width), BF),
            "att_f": vm((z.att_pad, toks), F32),
            "att_t": vm((heads * hd, toks), BF),
            "branch_s": vm((toks, width), F32),
            "grad_att": vm((heads * hd, toks), F32),
            "grad_mid": vm((toks, width), F32),
            "acc": vm((toks, width), F32),
            "gb_t": vm((toks, width), BF),
            "gb_s": vm((toks, width), BF),
            "part": vm((2, 2, pairs, hd, width), BF),
            "pair_recv": vm((2, pairs, hd, width), BF),
            "pair_sem": dma((2, 2)),
        }

        def both(name, n, shape, dtype, arrivals=1):
            scratch[name + "_send"] = vm((n,) + shape, dtype)
            scratch[name + "_recv"] = vm((n,) + shape, dtype)
            scratch[name + "_sem"] = dma((1 + arrivals,))

        both("kv", ns, (2 * hd, toks), BF, ns)
        both("qs", ns, (hd, toks), BF, ns)
        both("dq", ns, (hd, toks), BF, ns)
        both("dk", ns, (2 * hd, toks), BF, ns)
        both("at", ns, (hd, toks), BF)
        both("do", ns, (hd, toks), BF, ns)
        for name in ("tk", "cot", "gm"):
            both(name, nt, (width // 16, 128), BF)
        for name in ("aa", "ga", "ta"):
            both(name, nt, (z.att_pad // 16, 128), BF)
        both("y0", pairs, (hd, width), BF)
        both("x0", 4, (hd, width // 4), BF)
        both("x1", 4, (2 * pairs + 1, hd, 128), BF)
        both("y1", pairs, (hd, width // 4), BF)
        both("z0", nz, (hd // 3, 128), BF)
        both("z1", nz, (hd // 3, 128), BF)

        def rows(name, n, lines, dtype=F32):
            scratch[name + "_send"] = vm((lines, 128), dtype)
            scratch[name + "_recv"] = vm((n, lines, 128), dtype)
            scratch[name + "_sem"] = dma((2,))

        both("ex", 4, (16, 128), F32)
        rows("es", ns, z.early)
        rows("ez", nz, 16, BF)
        rows("ea", 4, 16)
        rows("ls", ns, z.late)
        rows("lx", 4, z.late)
        rows("lz", nz, z.late, BF)

        ins = [v + "_in" for v in ("tok", "cot", "val", "tab_s", "gn_s", "tab_t", "gn_t")]
        ins += ["qkv_s", "out_s", "qkv_t", "out_t"]
        names = ["mixed", "tgrad", "gos", "got", "tabs"]
        outs = [v + "_out" for v in names]
        shapes = [
            jax.ShapeDtypeStruct((toks, width), BF),
            jax.ShapeDtypeStruct((toks, width), BF),
            jax.ShapeDtypeStruct((width // 4 // nz, hd), F32),
            jax.ShapeDtypeStruct((width // 4 // nz, hd), F32),
            jax.ShapeDtypeStruct((3, 2, width), F32),
        ]
        for name, shape in zip(names, shapes):
            scratch[name] = vm(shape.shape, shape.dtype)
        scratch["o_sem"] = dma((5,))
        vmem = pl.BlockSpec(memory_space=pltpu.VMEM)
        anywhere = pl.BlockSpec(memory_space=pl.ANY)
        results = pl.pallas_call(
            functools.partial(kernel, z, ins + outs + list(scratch)),
            out_shape=shapes,
            in_specs=[anywhere] * 11,
            out_specs=[anywhere] * 5,
            scratch_shapes=list(scratch.values()),
            compiler_params=pltpu.CompilerParams(
                collective_id=0, has_side_effects=True, vmem_limit_bytes=62 * 1024 * 1024
            ),
        )(
            tokens.reshape(toks, width),
            cotangent.reshape(toks, width),
            validity.reshape(ns, toks),
            table_space,
            gains_space,
            table_time,
            gains_time,
            qkv_space.T,
            out_space,
            qkv_time.T,
            out_time,
        )
        mixed, tgrad, gos, got, tabs = pl.pallas_call(
            hand_on,
            out_shape=[jax.ShapeDtypeStruct(v.shape, v.dtype) for v in results],
            in_specs=[anywhere] * 5,
            out_specs=[anywhere] * 5,
            scratch_shapes=[vm(v.shape, v.dtype) for v in results] + [dma((5,)), dma((5,))],
        )(*results)
        shape = tokens.shape
        return mixed.reshape(shape), tgrad.reshape(shape), gos.T, got.T, tabs.transpose(1, 0, 2)

    spread = P("dp", "tm", "space", None)
    return jax.shard_map(
        on_device,
        mesh=mesh,
        in_specs=(spread,) + (P(),) * 9 + (spread,),
        out_specs=(spread, spread, P("space", ("dp", "tm")), P("space", ("dp", "tm")), P()),
        check_vma=False,
    )
```

```python
import functools

import jax
import jax.numpy as jnp
from jax import lax
from jax.experimental import pallas as pl
from jax.experimental.pallas import tpu as pltpu
from jax.sharding import PartitionSpec as P

MESH = pl.DeviceIdType.MESH
BF = jnp.bfloat16
F32 = jnp.float32
EPSILON = 1e-6
LOG2E = 1.4426950408889634

NN = (((1,), (0,)), ((), ()))
NT = (((1,), (1,)), ((), ()))
TN = (((0,), (0,)), ((), ()))


def dot(a, b, dims=NN):
    return lax.dot_general(a, b, dims, preferred_element_type=F32)


def mean(v):
    return jnp.mean(v, axis=-1, keepdims=True)


def norm(values):
    centred = values - mean(values)
    inv_std = lax.rsqrt(mean(centred * centred) + EPSILON)
    return centred * inv_std, inv_std


def feature_mean(v):
    return jnp.mean(v, axis=-2, keepdims=True)


def rms_scale(raw):
    return lax.rsqrt(feature_mean(raw * raw) + EPSILON)


def rms_back(grad, raw):
    inv = rms_scale(raw)
    return inv * (grad - raw * (inv * inv) * feature_mean(grad * raw))


def modulate_back(grad, normed, inv_std, table):
    grad_norm = grad * (1.0 + table[1:2, :])
    grad_in = inv_std * (grad_norm - mean(grad_norm) - normed * mean(grad_norm * normed))
    shift = jnp.sum(grad, axis=0, keepdims=True)
    scale = jnp.sum(grad * normed, axis=0, keepdims=True)
    return grad_in, shift, scale


class Sizes:
    pass


def to_blocks(rows):
    n, width = rows.shape[0] // 8, rows.shape[1]
    cube = rows.reshape(n, 8, width)
    return jnp.concatenate([cube[:, :, c : c + 128] for c in range(0, width, 128)], axis=1).astype(BF)


def from_blocks(blocks):
    n, lines, _ = blocks.shape
    cube = blocks.astype(F32)
    full = jnp.concatenate([cube[:, c : c + 8, :] for c in range(0, lines, 8)], axis=2)
    return full.reshape(n * 8, lines * 16)


def to_lines(rows, lines):
    parts = [r[:, c : c + 128] for r in rows for c in range(0, rows[0].shape[1], 128)]
    if lines > len(parts):
        parts.append(jnp.zeros((lines - len(parts), 128), F32))
    return jnp.concatenate(parts, axis=0)


def from_lines(lines, r, n):
    return jnp.concatenate([lines[n * r + c : n * r + c + 1, :] for c in range(n)], axis=1)


def kernel(z, names, *refs):
    r = Sizes()
    for name, ref in zip(names, refs):
        setattr(r, name, ref)
    heads, hd, width, toks, ns, nt, nz = (
        z.heads, z.hd, z.width, z.toks, z.ns, z.nt, z.nz,
    )
    att_w = heads * hd
    hp, pair_w, np_, two = z.hp, 6 * hd, heads // 2, 2 * toks
    scaling = hd ** (-0.5)
    power = scaling * LOG2E
    dp = lax.axis_index("dp")
    tm = lax.axis_index("tm")
    sp = lax.axis_index("space")
    core, y = sp % 2, sp // 2
    sibling = sp + 1 - 2 * core
    x_lo, zz = tm // nz, tm % nz
    x = dp * 2 + x_lo
    nx = 4
    ny = ns // 2

    def remote(src, dst, send_sem, recv_sem, device):
        return pltpu.make_async_remote_copy(
            src_ref=src, dst_ref=dst, send_sem=send_sem, recv_sem=recv_sem,
            device_id=device, device_id_type=MESH,
        )

    groups = {
        "space": (ns, sp, lambda j: (dp, tm, j)),
        "tm": (nt, tm, lambda j: (dp, j, sp)),
        "y": (ny, y, lambda j: (dp, tm, j * 2 + core)),
        "x": (nx, x, lambda j: (j // 2, (j % 2) * nz + zz, sp)),
        "z": (nz, zz, lambda j: (dp, x_lo * nz + j, sp)),
    }

    def exchange(group, src_of, recv, sems, d, each=False):
        n, me, device = groups[group]
        j = (me + d) % n
        arrived = sems.at[1 + me] if each else sems.at[1]
        return remote(src_of(j), recv.at[me], sems.at[0], arrived, device(j))

    def whole(group, src_of, recv, sems, each=False):
        n, me, device = groups[group]
        part = recv.at[pl.ds(0, n - 1)]
        return remote(part, part, sems.at[0], sems.at[1], device((me + 1) % n))

    ring = [4, 3, 5, 2, 6, 1, 7]
    order = {
        "space": ring,
        "z": ring,
        "x": [2, 1, 3],
        "y": [2, 1, 3],
        "tm": [d + h for d in ring for h in (0, nz)] + [nz],
    }

    def start_all(group, src_of, recv, sems, each=False):
        for d in order[group]:
            exchange(group, src_of, recv, sems, d, each).start()

    def start_to(args, j):
        n, me, _ = groups[args[0]]
        exchange(*args[:4], (j - me + n) % n, *args[4:]).start()

    def wait_from(group, src_of, recv, sems, each, j):
        device = groups[group][2]
        remote(src_of(j), recv.at[j], sems.at[0], sems.at[1 + j], device(j)).wait_recv()

    def wait_all(*args):
        whole(*args).wait_recv()

    def wait_sent(*args):
        whole(*args).wait_send()

    barrier = pltpu.get_barrier_semaphore()

    def signal(device):
        pl.semaphore_signal(barrier, inc=1, device_id=device, device_id_type=MESH)

    def greet(group):
        n, me, device = groups[group]
        for d in order[group]:
            signal(device((me + d) % n))

    greet("space")

    pair_order = [(y + d) % np_ for d in (2, 1, 3, 0)]

    def rows_of(b):
        return pl.ds(pl.multiple_of(b * pair_w, pair_w), pair_w)

    results = [
        pltpu.make_async_copy(src, dst, r.o_sem.at[i])
        for i, (src, dst) in enumerate(
            [
                (r.mixed, r.mixed_out),
                (r.tgrad, r.tgrad_out),
                (r.gos, r.gos_out),
                (r.got, r.got_out),
                (r.tabs, r.tabs_out),
            ]
        )
    ]
    pair_copies = [
        pltpu.make_async_copy(r.qkv_s.at[rows_of(b)], r.wqs.at[rows_of(b)], r.q_sem.at[i])
        for i, b in enumerate(pair_order)
    ]
    copies = {
        name: pltpu.make_async_copy(src, dst, r.w_sem.at[i])
        for i, (name, src, dst) in enumerate(
            [
                ("tok", r.tok_in, r.tok),
                ("tab_s", r.tab_s_in, r.tab_s),
                ("gn_s", r.gn_s_in, r.gn_s),
                ("val", r.val_in, r.val),
                ("cot", r.cot_in, r.cot),
                ("tab_t", r.tab_t_in, r.tab_t),
                ("gn_t", r.gn_t_in, r.gn_t),
                ("wos", r.out_s, r.wos),
                ("wot", r.out_t, r.wot),
                ("wqt", r.qkv_t, r.wqt),
            ]
        )
    }
    for name in ("tok", "tab_s", "gn_s"):
        copies[name].start()
    pair_copies[0].start()
    greet("tm")
    other = 1 - dp
    signal((other, tm, sp))
    signal((other, (1 - x_lo) * nz + zz, sp))
    for copy in pair_copies[1:]:
        copy.start()
    for name in ("val", "cot", "tab_t", "gn_t", "wos", "wot", "wqt"):
        copies[name].start()

    copies["tok"].wait()
    copies["tab_s"].wait()
    tokens = r.tok[...].astype(F32)
    table_s = r.tab_s[...]
    normed, _ = norm(tokens)
    shifted = (normed * (1.0 + table_s[1:2, :]) + table_s[0:1, :]).astype(BF)
    r.shift_s[...] = shifted

    def gain_columns(ref):
        g = ref[...]
        return [jnp.broadcast_to(g[i : i + 1, :], (toks, hd)).T for i in range(2)]

    copies["gn_s"].wait()
    gain_s = gain_columns(r.gn_s)
    pad_rows = jnp.zeros((hp - hd, toks), F32)
    first_row = lax.broadcasted_iota(jnp.int32, (hp - hd, toks), 0) == 0

    def padded(part):
        return jnp.concatenate([part, pad_rows], axis=0)

    kv = ("space", lambda j: r.kv_send.at[j], r.kv_recv, r.kv_sem, True)
    qs = ("space", lambda j: r.qs_send.at[j], r.qs_recv, r.qs_sem, True)

    def project_pair(i, b):
        pair_copies[i].wait()
        raw = dot(r.shift_s[...], r.wqs[rows_of(b), :], NT).T
        r.raw_s[b] = raw
        cube = raw.reshape(6, hd, toks)
        for c in range(2):
            p0, p1, p2 = cube[3 * c], cube[3 * c + 1], cube[3 * c + 2]
            q = p0 * rms_scale(p0) * gain_s[0]
            k = p1 * rms_scale(p1) * gain_s[1]
            r.qs_send[2 * b + c] = q.astype(BF)
            r.kv_send[2 * b + c] = jnp.concatenate([k, p2], axis=0).astype(BF)

    def start_pair(args, i, b):
        if i < np_ - 1:
            start_to(args, 2 * b)
            start_to(args, 2 * b + 1)
        else:
            start_to(args, sibling)

    project_pair(0, pair_order[0])
    r.tk_send[...] = to_blocks(r.tok[...].astype(F32))
    r.tk_recv[tm] = r.tk_send[tm]
    tk = ("tm", lambda j: r.tk_send.at[j], r.tk_recv, r.tk_sem)
    pl.semaphore_wait(barrier, ns - 1 + nt - 1 + 2)
    start_pair(kv, 0, pair_order[0])
    start_all(*tk)
    for i in range(1, np_):
        project_pair(i, pair_order[i])
        start_pair(kv, i, pair_order[i])
    for i in range(np_):
        start_pair(qs, i, pair_order[i])
    r.kv_recv[sp] = r.kv_send[sp]
    r.qs_recv[sp] = r.qs_send[sp]

    copies["cot"].wait()
    r.cot_send[...] = to_blocks(r.cot[...].astype(F32))
    r.cot_recv[tm] = r.cot_send[tm]
    ct = ("tm", lambda j: r.cot_send.at[j], r.cot_recv, r.cot_sem)
    start_all(*ct)
    copies["val"].wait()
    own_row = r.val[pl.ds(sp, 1), :].astype(F32)
    row_id = lax.broadcasted_iota(jnp.int32, (toks, toks), 0)
    col_id = lax.broadcasted_iota(jnp.int32, (toks, toks), 1)
    own = jnp.broadcast_to(own_row, (toks, toks))
    mask_s = jnp.sum(jnp.where(row_id == col_id, own, 0.0), axis=1, keepdims=True)
    mask_t = jnp.sum(jnp.where(tm * 8 + row_id % 8 == col_id, own, 0.0), axis=1, keepdims=True)


    def unpack(j):
        block = r.kv_recv[j].astype(F32)
        at = pl.ds(pl.multiple_of(j * toks, toks), toks)
        keys, values = block[:hd, :], block[hd:, :]
        bias = jnp.where(r.val[pl.ds(j, 1), :] > 0, 0.0, -1e30)
        r.k_t[:, at] = padded(keys).astype(BF)
        r.v_t[:, at] = padded(values).astype(BF)
        r.k_ref[at, :] = jnp.concatenate([keys, jnp.where(first_row, bias, 0.0)], axis=0).T.astype(BF)
        r.v_ref[at, :] = padded(values).T.astype(BF)

    unpack(sp)
    for b in pair_order[::-1]:
        for j in [sibling] if b is pair_order[-1] else [2 * b, 2 * b + 1]:
            wait_from(*kv, j)
            unpack(j)

    at = ("space", lambda j: r.at_send.at[j], r.at_recv, r.at_sem)

    def two_of(b):
        return pl.ds(pl.multiple_of(b * two, two), two)

    ones = jnp.where(lax.broadcasted_iota(jnp.int32, (hp - hd, two), 0) == 0, 1.0, 0.0)

    def scores_of(i, b):
        for j in [sibling] if i == 0 else [2 * b, 2 * b + 1]:
            wait_from(*qs, j)
        q = jnp.concatenate([r.qs_recv[2 * b + c].astype(F32) for c in range(2)], axis=1)
        r.q_t[:, two_of(b)] = jnp.concatenate([q, ones], axis=0).astype(BF)
        return dot(r.k_ref[...], r.q_t[:, two_of(b)])

    attend_order = [(y + d) % np_ for d in (0, 2, 1, 3)]
    following = scores_of(0, attend_order[0])
    for i, b in enumerate(attend_order):
        scores = following
        top = jnp.max(scores, axis=0, keepdims=True)
        if i < np_ - 1:
            following = scores_of(i + 1, attend_order[i + 1])
        exps = jnp.exp2(scores * power - top * power)
        inverse = 1.0 / jnp.sum(exps, axis=0, keepdims=True)
        exps = exps.astype(BF)
        r.prob[b] = exps
        out = dot(r.v_t[...], exps) * inverse
        r.inverse[b] = inverse
        r.o_ref[b] = out
        for c in range(2):
            r.at_send[2 * b + c] = out[:hd, toks * c : toks * (c + 1)].astype(BF)
        start_pair(at, np_ - 1 if i == 0 else 0, b)
    r.at_recv[sp] = r.at_send[sp]
    wait_all(*at)
    fill = jnp.zeros((z.att_pad - att_w, toks), F32)

    att = jnp.concatenate([r.at_recv[h].astype(F32) for h in range(heads)] + [fill], axis=0).T
    r.aa_send[...] = to_blocks(att)
    r.aa_recv[tm] = r.aa_send[tm]
    aa = ("tm", lambda j: r.aa_send.at[j], r.aa_recv, r.aa_sem)
    start_all(*aa)
    copies["wos"].wait()
    branch = dot(att[:, :att_w].astype(BF), r.wos[...])
    r.mid_o[...] = (r.tok[...].astype(F32) + mask_s * table_s[2:3, :] * branch).astype(BF)

    pair = (dp, tm, sibling)

    def pair_copy(a):
        return remote(
            r.part.at[a, 1 - core], r.pair_recv.at[a], r.pair_sem.at[0, a], r.pair_sem.at[1, a], pair
        )

    def partial_grad(a, att, grad_branch, dims=NN):
        full = dot(att, grad_branch, dims)
        for h in range(heads):
            r.part[a, h % 2, h // 2] = full[hd * h : hd * (h + 1), :].astype(BF)
        pair_copy(a).start()

    def rs_args(kind, a):
        send, recv, sems = (getattr(r, kind + str(a) + end) for end in ("_send", "_recv", "_sem"))
        return (kind, lambda j: send.at[j], recv, sems)

    def total(ref, n):
        value = ref[0].astype(F32)
        for j in range(1, n):
            value = value + ref[j].astype(F32)
        return value

    quarter = width // nx
    rest = quarter - 256

    def rs_y0():
        pair_copy(0).wait_recv()
        for b in range(ny):
            r.y0_send[b] = (r.part[0, core, b].astype(F32) + r.pair_recv[0, b].astype(F32)).astype(BF)
        r.y0_recv[y] = r.y0_send[y]
        start_all(*rs_args("y", 0))

    def rs_x0():
        wait_all(*rs_args("y", 0))
        value = total(r.y0_recv, ny)
        for j in range(nx):
            r.x0_send[j] = value[:, quarter * j : quarter * (j + 1)].astype(BF)
        r.x0_recv[x] = r.x0_send[x]
        start_all(*rs_args("x", 0))

    def rs_x1():
        pair_copy(1).wait_recv()
        value = [r.part[1, core, b].astype(F32) + r.pair_recv[1, b].astype(F32) for b in range(ny)]
        for j in range(nx):
            cols = [v[:, quarter * j : quarter * (j + 1)] for v in value]
            for b in range(ny):
                r.x1_send[j, 2 * b] = cols[b][:, :128].astype(BF)
                r.x1_send[j, 2 * b + 1] = cols[b][:, 128:256].astype(BF)
            r.x1_send[j, 2 * ny] = jnp.concatenate([v[:, 256:] for v in cols], axis=1).astype(BF)
        r.x1_recv[x] = r.x1_send[x]
        start_all(*rs_args("x", 1))

    def rs_y1():
        wait_all(*rs_args("x", 1))
        value = total(r.x1_recv, nx)
        for b in range(ny):
            tail = value[2 * ny][:, rest * b : rest * (b + 1)]
            r.y1_send[b] = jnp.concatenate([value[2 * b], value[2 * b + 1], tail], axis=1).astype(BF)
        r.y1_recv[y] = r.y1_send[y]
        start_all(*rs_args("y", 1))

    third = hd // 3
    own_w = quarter // nz

    def rs_z(a):
        wait_all(*rs_args("x" if a == 0 else "y", a))
        value = total(r.x0_recv, nx) if a == 0 else total(r.y1_recv, ny)
        _, send_of, recv, _ = rs_args("z", a)
        fill = jnp.zeros((third, 128 - 3 * own_w), F32)
        for j in range(nz):
            cols = value[:, own_w * j : own_w * (j + 1)]
            parts = [cols[third * c : third * (c + 1), :] for c in range(3)]
            send_of(j)[...] = jnp.concatenate(parts + [fill], axis=1).astype(BF)
        recv[zz] = send_of(zz)[...]
        start_all(*rs_args("z", a))

    def rs_end(a, out_ref):
        wait_all(*rs_args("z", a))
        value = total(rs_args("z", a)[2], nz)
        cols = [value[:, own_w * c : own_w * (c + 1)] for c in range(3)]
        out_ref[...] = jnp.concatenate(cols, axis=0).T

    def table_args(kind, k):
        send, recv, sems = (getattr(r, k + kind + end) for end in ("_send", "_recv", "_sem"))
        return ({"s": "space", "a": "x"}.get(kind, kind), lambda j: send, recv, sems)

    def table_start(kind, k, value):
        args = table_args(kind, k)
        send = getattr(r, k + kind + "_send")
        send[...] = value.astype(send.dtype)
        args[2][groups[args[0]][1]] = send[...]
        start_all(*args)

    def table_sum(kind, k):
        args = table_args(kind, k)
        wait_all(*args)
        value = args[2][0].astype(F32)
        for j in range(1, groups[args[0]][0]):
            value = value + args[2][j].astype(F32)
        return value

    copies["tab_t"].wait()
    table_t = r.tab_t[...]
    wait_all(*tk)
    r.tok_t[...] = from_blocks(r.tk_recv[...])
    wait_all(*ct)
    r.cot_t[...] = from_blocks(r.cot_recv[...])
    masked = r.cot_t[...] * mask_t
    grad_branch = (masked * table_t[2:3, :]).astype(BF)
    r.gb_t[...] = grad_branch
    copies["wot"].wait()
    r.grad_att[...] = dot(r.wot[...], grad_branch, NT)
    copies["wqt"].wait()
    copies["gn_t"].wait()
    gain_t = gain_columns(r.gn_t)
    for args in (kv, qs, at, tk, ct):
        wait_sent(*args)

    wait_all(*aa)
    att_s = from_blocks(r.aa_recv[...])[:, :att_w].astype(BF)
    r.att_s[...] = att_s
    branch_s = dot(att_s, r.wos[...])
    r.branch_s[...] = branch_s
    middle = r.tok_t[...] + mask_t * table_s[2:3, :] * branch_s
    r.mid[...] = middle.astype(BF)
    normed, inv_t = norm(r.mid[...].astype(F32))
    r.acc[...] = normed
    shifted = (normed * (1.0 + table_t[1:2, :]) + table_t[0:1, :]).astype(BF)
    raw = dot(shifted, r.wqt[...], NT).T.reshape(heads, 3, hd, toks)
    p0, p1, p2 = raw[:, 0], raw[:, 1], raw[:, 2]
    s0, s1 = rms_scale(p0), rms_scale(p1)
    r.p0[...] = p0
    r.p1[...] = p1
    q = p0 * s0 * gain_t[0][None]
    k = p1 * s1 * gain_t[1][None]
    q_f = [padded(q[h]) for h in range(heads)]
    k_f = [padded(k[h]) for h in range(heads)]
    v_f = [padded(p2[h]) for h in range(heads)]
    q_t, k_t, v_t = ([v.astype(BF) for v in part] for part in (q_f, k_f, v_f))
    same = (row_id % 8 == col_id % 8)[None]
    scores = jnp.stack([dot(k_f[h].T.astype(BF), q_t[h]) for h in range(heads)], axis=0)
    scores = jnp.where(same, scores, -1e30)
    exps = jnp.exp2((scores - jnp.max(scores, axis=1, keepdims=True)) * power)
    weights = exps * (1.0 / jnp.sum(exps, axis=1, keepdims=True))
    rounded = weights.astype(BF)
    att = jnp.concatenate([dot(v_t[h], rounded[h])[:hd, :] for h in range(heads)] + [fill], axis=0)
    r.att_f[...] = att
    r.att_t[...] = att[:att_w, :].astype(BF)
    partial_grad(0, r.att_t[...], r.gb_t[...])
    do_t = [padded(r.grad_att[hd * h : hd * (h + 1), :]).astype(BF) for h in range(heads)]
    dw = jnp.stack([dot(v_f[h].T.astype(BF), do_t[h]) for h in range(heads)], axis=0)
    ds = weights * (dw - jnp.sum(dw * weights, axis=1, keepdims=True)) * scaling
    ds = ds.astype(BF)

    def stacked(parts):
        return jnp.stack([v[:hd, :] for v in parts], axis=0).astype(BF).astype(F32)

    dq = stacked([dot(k_t[h], ds[h]) for h in range(heads)])
    dk = stacked([dot(q_t[h], ds[h], NT) for h in range(heads)])
    dv = stacked([dot(do_t[h], rounded[h], NT) for h in range(heads)])
    dq = rms_back(dq * gain_t[0][None], r.p0[...])
    dk = rms_back(dk * gain_t[1][None], r.p1[...])
    grad_raw = jnp.stack([dq, dk, dv], axis=1).reshape(3 * att_w, toks).astype(BF)
    grad_shifted = dot(grad_raw, r.wqt[...], TN)
    grad_in, shift_t, scale_t = modulate_back(grad_shifted, r.acc[...], inv_t, table_t)
    grad_mid = (r.cot_t[...] + grad_in).astype(BF).astype(F32)
    r.grad_mid[...] = grad_mid
    rs_y0()
    grad_branch = (grad_mid * mask_t * table_s[2:3, :]).astype(BF)
    r.gb_s[...] = grad_branch
    grad_att = dot(grad_branch, r.wos[...], NT)
    r.ga_send[...] = to_blocks(
        jnp.concatenate([grad_att, jnp.zeros((toks, z.att_pad - att_w), F32)], axis=1)
    )
    r.ga_recv[tm] = r.ga_send[tm]
    ga = ("tm", lambda j: r.ga_send.at[j], r.ga_recv, r.ga_sem)
    start_all(*ga)

    partial_grad(1, r.att_s[...], r.gb_s[...], TN)
    branch_t = dot(r.att_t[...], r.wot[...], TN)
    gate_t = jnp.sum(r.cot_t[...] * mask_t * branch_t, axis=0, keepdims=True)
    gate_s = jnp.sum(r.grad_mid[...] * mask_t * r.branch_s[...], axis=0, keepdims=True)
    r.gm_send[...] = to_blocks(r.grad_mid[...])
    r.gm_recv[tm] = r.gm_send[tm]
    gm = ("tm", lambda j: r.gm_send.at[j], r.gm_recv, r.gm_sem)
    r.ta_send[...] = to_blocks(r.att_f[...].T)
    r.ta_recv[tm] = r.ta_send[tm]
    ta = ("tm", lambda j: r.ta_send.at[j], r.ta_recv, r.ta_sem)
    rs_x1()
    wait_sent(*aa)

    wait_all(*ga)
    grad_att = from_blocks(r.ga_recv[...]).T
    for h in range(heads):
        r.do_send[h] = grad_att[hd * h : hd * (h + 1), :].astype(BF)
    r.do_recv[sp] = r.do_send[sp]
    do = ("space", lambda j: r.do_send.at[j], r.do_recv, r.do_sem, True)
    start_all(*do)
    early_rows = to_lines([shift_t, scale_t, gate_t, gate_s], z.early)

    lines = width // 128
    ex = ("x", lambda j: r.ex_send.at[j], r.ex_recv, r.ex_sem)

    def early_x():
        value = table_sum("s", "e")
        blank = jnp.zeros((16 - lines, 128), F32)
        for j in range(nx):
            r.ex_send[j] = jnp.concatenate([value[lines * j : lines * (j + 1), :], blank], axis=0)
        r.ex_recv[x] = r.ex_send[x]
        start_all(*ex)

    def early_z():
        wait_all(*ex)
        table_start("z", "e", r.ex_recv[0] + r.ex_recv[1] + r.ex_recv[2] + r.ex_recv[3])

    dqs = ("space", lambda j: r.dq_send.at[j], r.dq_recv, r.dq_sem, True)
    dks = ("space", lambda j: r.dk_send.at[j], r.dk_recv, r.dk_sem, True)
    back_order = [(y + d) % np_ for d in (0, 1, 3, 2)]
    for i, b in enumerate(back_order):
        for j in [sibling] if i == 0 else [2 * b, 2 * b + 1]:
            wait_from(*do, j)
        grad_out = jnp.concatenate([r.do_recv[2 * b + c].astype(F32) for c in range(2)], axis=1)
        grad_out = grad_out * (r.inverse[b] * scaling)
        grad_out = jnp.concatenate([grad_out, jnp.zeros((hp - hd, two), F32)], axis=0).astype(BF)
        shared = jnp.sum(grad_out.astype(F32) * r.o_ref[b], axis=0, keepdims=True)
        exps = r.prob[b]
        ds = (exps.astype(F32) * (dot(r.v_ref[...], grad_out) - shared)).astype(BF)
        dq = dot(r.k_t[...], ds)
        for c in range(2):
            r.dq_send[2 * b + c] = dq[:hd, toks * c : toks * (c + 1)].astype(BF)
        start_pair(dqs, np_ - 1 if i == 0 else 0, b)
        dv = dot(grad_out, exps, NT)
        dk = dot(r.q_t[:, two_of(b)], ds, NT)
        r.dv_t[...] = dv if i == 0 else r.dv_t[...] + dv
        r.dk_t[...] = dk if i == 0 else r.dk_t[...] + dk
        if i == 0:
            start_all(*gm)
        if i == 1:
            table_start("s", "e", early_rows)
        if i == 2:
            rs_x0()
            start_all(*ta)
    for j in range(ns):
        cols = slice(toks * j, toks * (j + 1))
        r.dk_send[j] = jnp.concatenate(
            [r.dk_t[:hd, cols], r.dv_t[:hd, cols] * (1.0 / scaling)], axis=0
        ).astype(BF)
    start_all(*dks)
    r.dq_recv[sp] = r.dq_send[sp]
    r.dk_recv[sp] = r.dk_send[sp]

    rs_y1()
    for args in (ga, do):
        wait_sent(*args)
    pair_copy(0).wait_send()
    pair_copy(1).wait_send()

    normed, inv_s = norm(r.tok[...].astype(F32))
    for i, b in enumerate(back_order):
        for j in [sibling] if i == 0 else [2 * b, 2 * b + 1]:
            wait_from(*dqs, j)
            wait_from(*dks, j)
        raw = r.raw_s[b].reshape(6, hd, toks)
        parts = []
        for c in range(2):
            dq = r.dq_recv[2 * b + c].astype(F32)
            dkv = r.dk_recv[2 * b + c].astype(F32)
            parts.append(rms_back(dq * gain_s[0], raw[3 * c]))
            parts.append(rms_back(dkv[:hd, :] * gain_s[1], raw[3 * c + 1]))
            parts.append(dkv[hd:, :])
        grad_raw = jnp.concatenate(parts, axis=0).astype(BF)
        share = dot(grad_raw, r.wqs[rows_of(b), :], TN)
        r.acc[...] = share if i == 0 else r.acc[...] + share
        if i == 0:
            early_x()
    grad_in, shift_s, scale_s = modulate_back(r.acc[...], normed, inv_s, table_s)
    table_start("s", "l", to_lines([shift_s, scale_s], z.late))
    rs_z(0)
    table_start("x", "l", table_sum("s", "l"))
    early_z()
    rs_z(1)
    wait_all(*gm)
    r.tgrad[...] = (from_blocks(r.gm_recv[...]) + grad_in).astype(BF)
    results[1].start()
    table_start("z", "l", table_sum("x", "l"))
    wait_all(*ta)
    branch = dot(from_blocks(r.ta_recv[...])[:, :att_w].astype(BF), r.wot[...])
    mixed = r.mid_o[...].astype(F32) + mask_s * table_t[2:3, :] * branch
    r.mixed[...] = mixed.astype(BF)
    results[0].start()
    for args in (dqs, dks, gm, ta, ex):
        wait_sent(*args)
    for a in range(2):
        wait_sent(*rs_args("x", a))
    for a in range(2):
        wait_sent(*rs_args("y", a))
    for args in [table_args("s", "e"), table_args("z", "e"), table_args("s", "l"), table_args("x", "l")]:
        wait_sent(*args)
    wait_sent(*rs_args("z", 0))
    table_start("a", "e", table_sum("z", "e"))
    rs_end(0, r.got)
    results[3].start()
    wait_all(*table_args("a", "e"))
    rs_end(1, r.gos)
    results[2].start()
    wait_sent(*rs_args("z", 1))
    wait_sent(*table_args("a", "e"))
    late = table_sum("z", "l")
    space_rows = [from_lines(late, 0, lines), from_lines(late, 1, lines), from_lines(r.ea_recv[3], 0, lines)]
    for i in range(3):
        r.tabs[i] = jnp.concatenate([space_rows[i], from_lines(r.ea_recv[i], 0, lines)], axis=0)
    results[4].start()
    wait_sent(*table_args("z", "l"))
    for copy in results:
        copy.wait()


def hand_on(*refs):
    n = (len(refs) - 2) // 3
    srcs, dsts, stages, (into, out) = refs[:n], refs[n : 2 * n], refs[2 * n : 3 * n], refs[3 * n :]
    first = [pltpu.make_async_copy(srcs[i], stages[i], into.at[i]) for i in range(n)]
    second = [pltpu.make_async_copy(stages[i], dsts[i], out.at[i]) for i in range(n)]
    for copy in first:
        copy.start()
    for i in range(n):
        first[i].wait()
        second[i].start()
    for copy in second:
        copy.wait()


def solution(mesh):
    nt, ns = mesh.shape["tm"], mesh.shape["space"]

    def on_device(
        tokens, validity, table_space, qkv_space, gains_space, out_space,
        table_time, qkv_time, gains_time, out_time, cotangent,
    ):
        z = Sizes()
        z.width = tokens.shape[3]
        z.toks = tokens.shape[2]
        z.hd = gains_space.shape[1]
        z.heads = out_space.shape[0] // z.hd
        z.ns, z.nt, z.nz = ns, nt, nt // 2
        z.hp = 80
        heads, hd, width, toks, nz, hp = z.heads, z.hd, z.width, z.toks, z.nz, z.hp
        qw, pairs, patches = 3 * heads * hd, ns // 2, ns * toks
        dma = pltpu.SemaphoreType.DMA
        vm = pltpu.VMEM
        z.att_pad = -(-heads * hd // 128) * 128
        z.early, z.late = 48, 32
        scratch = {
            "wqs": vm((qw, width), BF),
            "wos": vm((heads * hd, width), BF),
            "wqt": vm((qw, width), BF),
            "wot": vm((heads * hd, width), BF),
            "tok": vm((toks, width), BF),
            "cot": vm((toks, width), BF),
            "val": vm((ns, toks), jnp.int32),
            "tab_s": vm((3, width), F32),
            "tab_t": vm((3, width), F32),
            "gn_s": vm((2, hd), F32),
            "gn_t": vm((2, hd), F32),
            "q_sem": dma((pairs,)),
            "w_sem": dma((10,)),
            "shift_s": vm((toks, width), BF),
            "raw_s": vm((pairs, 6 * hd, toks), F32),
            "p0": vm((heads, hd, toks), F32),
            "p1": vm((heads, hd, toks), F32),
            "q_t": vm((hp, patches), BF),
            "k_t": vm((hp, patches), BF),
            "v_t": vm((hp, patches), BF),
            "k_ref": vm((patches, hp), BF),
            "v_ref": vm((patches, hp), BF),
            "prob": vm((pairs, patches, 2 * toks), BF),
            "inverse": vm((pairs, 1, 2 * toks), F32),
            "o_ref": vm((pairs, hp, 2 * toks), F32),
            "dk_t": vm((hp, patches), F32),
            "dv_t": vm((hp, patches), F32),
            "att_s": vm((toks, heads * hd), BF),
            "mid": vm((toks, width), BF),
            "mid_o": vm((toks, width), BF),
            "att_f": vm((z.att_pad, toks), F32),
            "att_t": vm((heads * hd, toks), BF),
            "branch_s": vm((toks, width), F32),
            "tok_t": vm((toks, width), F32),
            "cot_t": vm((toks, width), F32),
            "grad_att": vm((heads * hd, toks), F32),
            "grad_mid": vm((toks, width), F32),
            "acc": vm((toks, width), F32),
            "gb_t": vm((toks, width), BF),
            "gb_s": vm((toks, width), BF),
            "part": vm((2, 2, pairs, hd, width), BF),
            "pair_recv": vm((2, pairs, hd, width), BF),
            "pair_sem": dma((2, 2)),
        }

        def both(name, n, shape, dtype, arrivals=1):
            scratch[name + "_send"] = vm((n,) + shape, dtype)
            scratch[name + "_recv"] = vm((n,) + shape, dtype)
            scratch[name + "_sem"] = dma((1 + arrivals,))

        both("kv", ns, (2 * hd, toks), BF, ns)
        both("qs", ns, (hd, toks), BF, ns)
        both("dq", ns, (hd, toks), BF, ns)
        both("dk", ns, (2 * hd, toks), BF, ns)
        both("at", ns, (hd, toks), BF)
        both("do", ns, (hd, toks), BF, ns)
        for name in ("tk", "cot", "gm"):
            both(name, nt, (width // 16, 128), BF)
        for name in ("aa", "ga", "ta"):
            both(name, nt, (z.att_pad // 16, 128), BF)
        both("y0", pairs, (hd, width), BF)
        both("x0", 4, (hd, width // 4), BF)
        both("x1", 4, (2 * pairs + 1, hd, 128), BF)
        both("y1", pairs, (hd, width // 4), BF)
        both("z0", nz, (hd // 3, 128), BF)
        both("z1", nz, (hd // 3, 128), BF)

        def rows(name, n, lines, dtype=F32):
            scratch[name + "_send"] = vm((lines, 128), dtype)
            scratch[name + "_recv"] = vm((n, lines, 128), dtype)
            scratch[name + "_sem"] = dma((2,))

        both("ex", 4, (16, 128), F32)
        rows("es", ns, z.early, BF)
        rows("ez", nz, 16, BF)
        rows("ea", 4, 16)
        rows("ls", ns, z.late)
        rows("lx", 4, z.late)
        rows("lz", nz, z.late, BF)

        ins = [v + "_in" for v in ("tok", "cot", "val", "tab_s", "gn_s", "tab_t", "gn_t")]
        ins += ["qkv_s", "out_s", "qkv_t", "out_t"]
        names = ["mixed", "tgrad", "gos", "got", "tabs"]
        outs = [v + "_out" for v in names]
        shapes = [
            jax.ShapeDtypeStruct((toks, width), BF),
            jax.ShapeDtypeStruct((toks, width), BF),
            jax.ShapeDtypeStruct((width // 4 // nz, hd), F32),
            jax.ShapeDtypeStruct((width // 4 // nz, hd), F32),
            jax.ShapeDtypeStruct((3, 2, width), F32),
        ]
        for name, shape in zip(names, shapes):
            scratch[name] = vm(shape.shape, shape.dtype)
        scratch["o_sem"] = dma((5,))
        vmem = pl.BlockSpec(memory_space=pltpu.VMEM)
        anywhere = pl.BlockSpec(memory_space=pl.ANY)
        results = pl.pallas_call(
            functools.partial(kernel, z, ins + outs + list(scratch)),
            out_shape=shapes,
            in_specs=[anywhere] * 11,
            out_specs=[anywhere] * 5,
            scratch_shapes=list(scratch.values()),
            compiler_params=pltpu.CompilerParams(
                collective_id=0, has_side_effects=True, vmem_limit_bytes=62 * 1024 * 1024
            ),
        )(
            tokens.reshape(toks, width),
            cotangent.reshape(toks, width),
            validity.reshape(ns, toks),
            table_space,
            gains_space,
            table_time,
            gains_time,
            qkv_space.T,
            out_space,
            qkv_time.T,
            out_time,
        )
        mixed, tgrad, gos, got, tabs = pl.pallas_call(
            hand_on,
            out_shape=[jax.ShapeDtypeStruct(v.shape, v.dtype) for v in results],
            in_specs=[anywhere] * 5,
            out_specs=[anywhere] * 5,
            scratch_shapes=[vm(v.shape, v.dtype) for v in results] + [dma((5,)), dma((5,))],
        )(*results)
        shape = tokens.shape
        return mixed.reshape(shape), tgrad.reshape(shape), gos.T, got.T, tabs.transpose(1, 0, 2)

    spread = P("dp", "tm", "space", None)
    return jax.shard_map(
        on_device,
        mesh=mesh,
        in_specs=(spread,) + (P(),) * 9 + (spread,),
        out_specs=(spread, spread, P("space", ("dp", "tm")), P("space", ("dp", "tm")), P()),
        check_vma=False,
    )
```
